128 devices in a mesh: rep: 8 (over z_lo, y), fsdp: 16 (over x, z_hi, core).
Axes of the slice: x: 4, y: 4, z: 4 (z_hi: 2, z_lo: 2; z = z_hi * 2 + z_lo), core: 2. Of those that a mesh axis runs over, the one named last changes fastest.
Arguments:
- attn_out: bfloat16 [65536, 2048], P(('rep', 'fsdp')), may hold values from -6 to 6
- grad_out: bfloat16 [65536, 4608], P(('rep', 'fsdp')), may hold values from -6 to 6
- inner_w: bfloat16 [8, 2048, 4608], P('rep', 'fsdp'), may hold values from -6 to 6
- anchor: float32 [2048, 4608], P('fsdp', 'rep'), may hold values from -6 to 6
- momentum: float32 [2048, 4608], P('fsdp', 'rep'), may hold values from -4 to 4
- delayed: float32 [2048, 4608], P('fsdp', 'rep'), may hold values from -4 to 4
Outputs:
- input_grad: bfloat16 [65536, 2048], P(('rep', 'fsdp'))
- new_inner: bfloat16 [8, 2048, 4608], P('rep', 'fsdp')
- new_anchor: float32 [2048, 4608], P('fsdp', 'rep')
- new_momentum: float32 [2048, 4608], P('fsdp', 'rep')
- outer_grad: float32 [2048, 4608], P('fsdp', 'rep')
The draws below stay inside these ranges and needn't reach their ends.
All inputs are finite; a program needn't handle non-finite values.
Results may differ from the reference program's by a relative error of at most 0.015.
Values may be sent and summed in bfloat16 or wider, within the bound.
A program may use at most 256 MiB of HBM per device.

```python
import jax
import jax.numpy as jnp
from jax import lax

D = 4608
TOK_DEV = 512
HD = 2048
ROWS = 65536
N_REP = 8


def steps_of(rng, dims, cuts, low, largest):
    gain = 1.0
    for axis_at, shards_of in cuts:
        steps = jax.random.uniform(jax.random.fold_in(jax.random.fold_in(rng, 6), axis_at), (shards_of,), jnp.float32, low / len(cuts), largest / len(cuts))
        gain = gain * jnp.repeat(jnp.exp(steps), dims[axis_at] // shards_of).reshape((-1,) + (1,) * (len(dims) - 1 - axis_at))
    return gain


def bell_draw(key, dims, width, most, split=(), dtype=jnp.bfloat16):
    loudness = steps_of(key, dims, split, -0.22, 0.18) if split else 1.0
    result = jax.random.normal(key, dims, jnp.float32) * width * loudness
    return jnp.minimum(jnp.maximum(result, -most), most).astype(dtype)


def setup_inputs(seed: int = 0) -> dict:
    seeds = jax.random.split(jax.random.key(seed), 7)
    attn_out = bell_draw(seeds[0], (ROWS, HD), 1.0, 6.0, ((0, 128),))
    grad_out = bell_draw(seeds[1], (ROWS, D), 1.0, 6.0, ((0, 128),))
    inner_w = bell_draw(seeds[2], (N_REP, HD, D), 1.0, 6.0, ((0, 8), (1, 16)))
    anchor = bell_draw(seeds[3], (HD, D), 1.0, 6.0, ((0, 16), (1, 8)), jnp.float32)
    momentum = bell_draw(seeds[4], (HD, D), 0.5, 4.0, ((0, 16), (1, 8)), jnp.float32)
    delayed = bell_draw(seeds[5], (HD, D), 0.5, 4.0, ((0, 16), (1, 8)), jnp.float32)
    return dict(attn_out=attn_out, grad_out=grad_out, inner_w=inner_w, anchor=anchor, momentum=momentum, delayed=delayed)


def reference(attn_out, grad_out, inner_w, anchor, momentum, delayed):
    replicas = inner_w.shape[0]
    factor = D ** -0.5
    attn_blocks = attn_out.reshape(replicas, -1, TOK_DEV, attn_out.shape[1])
    grad_blocks = grad_out.reshape(replicas, -1, TOK_DEV, grad_out.shape[1])

    def replica_step(operands):
        attn_rep, grad_rep, weights = operands

        def add_block(running, blocks_pair):
            attn_block, grad_block = blocks_pair
            product_term = jnp.dot(attn_block.T, grad_block, preferred_element_type=jnp.float32) * factor
            product_term = lax.optimization_barrier(product_term.astype(jnp.bfloat16)).astype(jnp.float32)
            return running + product_term, None

        zeroes = jnp.zeros(weights.shape, jnp.float32)
        grad_sum, _ = lax.scan(add_block, zeroes, (attn_rep, grad_rep))
        flat_grad = grad_rep.reshape(-1, grad_rep.shape[2])
        cotangent = (jnp.dot(flat_grad, weights.T, preferred_element_type=jnp.float32) * factor).astype(jnp.bfloat16)
        stepped = (weights.astype(jnp.float32) - grad_sum).astype(jnp.bfloat16)
        return cotangent, stepped

    cotangent, stepped = lax.map(replica_step, (attn_blocks, grad_blocks, inner_w))
    summed = jnp.sum(stepped.astype(jnp.float32), axis=0)
    outer_grad = anchor - summed / replicas
    new_momentum = 0.9 * momentum + delayed
    new_anchor = anchor - 0.7 * (delayed + 0.9 * new_momentum)
    new_inner = (0.5 * new_anchor[None] + 0.5 * stepped.astype(jnp.float32)).astype(jnp.bfloat16)
    input_grad = cotangent.reshape(-1, cotangent.shape[2])
    return input_grad, new_inner, new_anchor, new_momentum, outer_grad
```

```python
import functools

import jax
import jax.numpy as jnp
from jax import lax
from jax.experimental import pallas as pl
from jax.experimental.pallas import tpu as pltpu
from jax.sharding import PartitionSpec as P

MESH = pl.DeviceIdType.MESH
BF = jnp.bfloat16
F32 = jnp.float32

BLK = 128
H = 64
TILE_N = 512
TILE_M = 256
PIECE = 576
WIDE = 640

AGX, AGF, AGZ, RS1, RSD, RS2, RSZ, SIBG, SIBA, IG = 0, 4, 6, 14, 18, 22, 26, 28, 29, 30
RAZ, RAY, RRY, RRZ, N_MSG = 38, 39, 45, 57, 59


def kernel(
    a_hbm, g_hbm, w_hbm, anchor_ref, mom_ref, del_ref,
    ig_hbm, ni_ref, na_ref, nm_ref, og_ref,
    w_all, g_all, a_all, a_t, part, rx1, rxd, rx2, rxz,
    ig_own, ig_tx, st, an_all, ry, tz, rzl, pad,
    send, recv, local,
):
    factor = g_hbm.shape[1] ** (-0.5)
    d = g_hbm.shape[1]
    tok = g_hbm.shape[0]
    rep = lax.axis_index("rep")
    fs = lax.axis_index("fsdp")
    x, zh, c = fs // 4, (fs // 2) % 2, fs % 2
    zl, y = rep // 4, rep % 4

    def at_x(k):
        return (x + k) % 4

    def fs_of(xx, zz, cc):
        return xx * 4 + zz * 2 + cc

    sib = (rep, fs_of(x, zh, 1 - c))
    zpeer = (rep, fs_of(x, 1 - zh, c))
    xpeer = {k: (rep, fs_of(at_x(k), zh, c)) for k in (1, 3)}
    ypeer = {k: (zl * 4 + (y + k) % 4, fs) for k in (1, 2, 3)}
    lpeer = ((1 - zl) * 4 + y, fs)

    def blk(k, zi):
        return at_x(k) * 2 + (zh if zi else 1 - zh)

    def msg(i, src, dst, dev):
        return pltpu.make_async_remote_copy(
            src_ref=src, dst_ref=dst, send_sem=send.at[i], recv_sem=recv.at[i],
            device_id=dev, device_id_type=MESH,
        )

    sent = []

    def go(i, src, dst, dev):
        m = msg(i, src, dst, dev)
        m.start()
        sent.append(m)

    def got(i, ref):
        msg(i, ref, ref, sib).wait_recv()

    def rows(h):
        return pl.ds(h * H, H)

    def strips(n, body):
        def step(i, carry):
            body(pl.multiple_of(i * 16, 16))
            return carry

        lax.fori_loop(0, n // 16, step, 0)

    own = blk(0, 1)

    load_g = pltpu.make_async_copy(g_hbm, g_all.at[pl.ds(0, tok)], local.at[0])
    load_a = pltpu.make_async_copy(a_hbm, a_all.at[pl.ds(0, tok)], local.at[1])
    load_w = pltpu.make_async_copy(w_hbm.at[0], w_all.at[own], local.at[2])

    barrier = pltpu.get_barrier_semaphore()
    peers = [sib, zpeer, xpeer[1], xpeer[3], ypeer[1], ypeer[2], ypeer[3], lpeer]
    for p in peers:
        pl.semaphore_signal(barrier, inc=1, device_id=p, device_id_type=MESH)
    load_g.start()
    load_a.start()
    load_w.start()
    pl.semaphore_wait(barrier, len(peers))

    go(SIBA, a_hbm, a_all.at[pl.ds(tok, tok)], sib)
    go(SIBG, g_hbm, g_all.at[pl.ds(tok, tok)], sib)
    for h in (0, 1):
        for way, k in ((0, 1), (1, 3)):
            hh = h if way == 0 else 1 - h
            go(AGX + way * 2 + hh, w_hbm.at[0, rows(hh)], w_all.at[own, rows(hh)], xpeer[k])
        go(AGZ + h, w_hbm.at[0, rows(h)], w_all.at[own, rows(h)], zpeer)

    pad[...] = jnp.zeros_like(pad)

    def outer(r):
        sl = pl.ds(r, 16)
        nm = 0.9 * mom_ref[sl, :] + del_ref[sl, :]
        na = anchor_ref[sl, :] - 0.7 * (del_ref[sl, :] + 0.9 * nm)
        nm_ref[sl, :] = nm
        na_ref[sl, :] = na
        pad[sl, pl.ds(0, PIECE)] = na
        v = pad[sl, :]
        odd = (y % 2) == 1
        an_all[rep, sl, :] = jnp.where(odd, pltpu.roll(v, WIDE - PIECE, 1), v).astype(BF)

    strips(BLK, outer)
    go(RAZ, an_all.at[rep], an_all.at[rep], lpeer)
    for k in (1, 2, 3):
        go(RAY + k - 1, an_all.at[rep], an_all.at[rep], ypeer[k])

    load_a.wait()
    load_g.wait()
    got(SIBA, a_hbm)
    got(SIBG, g_hbm)

    def products(k):
        for zi in (0, 1):
            col = pl.multiple_of(fs_of(at_x(k), zh if zi else 1 - zh, c) * BLK, BLK)
            a_t[pl.ds(zi * BLK, BLK), :] = a_all[:, pl.ds(col, BLK)].T

        def step(n, carry):
            cols = pl.ds(pl.multiple_of(n * TILE_N, TILE_N), TILE_N)
            r = jnp.dot(a_t[...], g_all[:, cols], preferred_element_type=F32) * factor
            part[k, 0, :, cols] = r[:BLK].astype(BF)
            part[k, 1, :, cols] = r[BLK:].astype(BF)
            return carry

        lax.fori_loop(0, d // TILE_N, step, 0)

    def first(zi):
        for h, k in ((0, 1), (1, 3)):
            go(RS1 + zi * 2 + h, part.at[2, zi, rows(h)], rx1.at[zi, h], xpeer[k])

    def direct(zi):
        for h, k in ((1, 1), (0, 3)):
            go(RSD + zi * 2 + h, part.at[k, zi, rows(h)], rxd.at[zi, h], xpeer[k])

    def second(zi):
        for h, k in ((0, 1), (1, 3)):
            got(RS1 + zi * 2 + h, rx1.at[zi, h])

            def body(r, h=h, k=k):
                sl = pl.ds(h * H + r, 16)
                v = part[k, zi, sl, :].astype(F32) + rx1[zi, h, pl.ds(r, 16), :].astype(F32)
                part[k, zi, sl, :] = v.astype(BF)

            strips(H, body)
            go(RS2 + zi * 2 + h, part.at[k, zi, rows(h)], rx2.at[zi, h], xpeer[k])

    def input_grad(slot, k, zi):
        b = blk(k, zi)

        def tile(r):
            sl = pl.ds(r, TILE_M)
            return (
                lax.dot_general(
                    g_all[sl, :], w_all[b], (((1,), (1,)), ((), ())), preferred_element_type=F32
                )
                * factor
            ).astype(BF)

        def to_sib(i, carry):
            r = pl.multiple_of(i * TILE_M, TILE_M)
            ig_tx[slot, pl.ds(r, TILE_M), :] = tile(tok + r)
            return carry

        def to_own(i, carry):
            r = pl.multiple_of(i * TILE_M, TILE_M)
            ig_own[slot, pl.ds(r, TILE_M), :] = tile(r)
            return carry

        col = pl.multiple_of(fs_of(at_x(k), zh if zi else 1 - zh, c) * BLK, BLK)
        there = ig_hbm.at[:, pl.ds(col, BLK)]
        lax.fori_loop(0, tok // TILE_M, to_sib, 0)
        go(IG + slot, ig_tx.at[slot], there, sib)
        lax.fori_loop(0, tok // TILE_M, to_own, 0)
        cp = pltpu.make_async_copy(ig_own.at[slot], there, local.at[3 + slot])
        cp.start()
        stores.append(cp)

    stores = []

    products(2)
    first(0)
    products(1)
    products(3)
    direct(0)

    for way, k in ((0, 3), (1, 1)):
        for h in (0, 1):
            got(AGX + way * 2 + h, w_all.at[blk(k, 1), rows(h)])
            ref = w_all.at[blk(k, 1), rows(h)]
            go(AGZ + 2 + way * 2 + h, ref, ref, zpeer)

    products(0)
    load_w.wait()
    second(0)
    for way, k in ((0, 3), (1, 1)):
        ref = w_all.at[blk(k, 1), rows(way)]
        go(AGF + way, ref, ref, xpeer[1 if way == 0 else 3])
    first(1)
    direct(1)

    got(RAZ, an_all.at[lpeer[0]])
    for k in (1, 2, 3):
        ref = an_all.at[lpeer[0]]
        go(RAY + 3 + k - 1, ref, ref, ypeer[k])

    input_grad(0, 0, 1)
    input_grad(1, 1, 1)
    input_grad(2, 3, 1)

    for h in (0, 1):
        got(RSD + h, rxd.at[0, h])
        got(RS2 + h, rx2.at[0, h])

        def body(r, h=h):
            sl = pl.ds(h * H + r, 16)
            v = (
                part[0, 0, sl, :].astype(F32)
                + rxd[0, h, pl.ds(r, 16), :].astype(F32)
                + rx2[0, h, pl.ds(r, 16), :].astype(F32)
            )
            part[0, 0, sl, :] = v.astype(BF)

        strips(H, body)
        go(RSZ + h, part.at[0, 0, rows(h)], rxz.at[h], zpeer)

    for h in (0, 1):
        ref = w_all.at[blk(2, 1), rows(h)]
        got(AGF + h, ref)
        go(AGZ + 6 + h, ref, ref, zpeer)

    second(1)
    input_grad(3, 2, 1)
    for h in (0, 1):
        got(AGZ + h, w_all.at[blk(0, 0), rows(h)])
    input_grad(4, 0, 0)
    for slot, (way, k) in ((5, (0, 3)), (6, (1, 1))):
        for h in (0, 1):
            got(AGZ + 2 + way * 2 + h, w_all.at[blk(k, 0), rows(h)])
        input_grad(slot, k, 0)

    def piece(zz, yy):
        return pl.multiple_of(zz * 2304 + (yy // 2) * 1152 + (yy % 2) * 512, 128)

    for h in (0, 1):
        got(RSD + 2 + h, rxd.at[1, h])
        got(RSZ + h, rxz.at[h])
        got(RS2 + 2 + h, rx2.at[1, h])

        def body(r, h=h):
            sl = pl.ds(h * H + r, 16)
            hs = pl.ds(r, 16)
            v = (
                (part[0, 1, sl, :].astype(F32) + rxd[1, h, hs, :].astype(F32))
                + rx2[1, h, hs, :].astype(F32)
            ) + rxz[h, hs, :].astype(F32)
            st[sl, :] = (w_all[own, sl, :].astype(F32) - v).astype(BF)

        strips(H, body)
        for k in (1, 2, 3):
            for zz in (0, 1):
                col = piece(zz, (y + k) % 4)
                go(
                    RRY + h * 6 + (k - 1) * 2 + zz,
                    st.at[rows(h), pl.ds(col, WIDE)], ry.at[k - 1, zz, rows(h)], ypeer[k],
                )

    for h in (0, 1):
        got(AGZ + 6 + h, w_all.at[blk(2, 0), rows(h)])
    input_grad(7, 2, 0)

    for k in (1, 2, 3):
        got(RAY + k - 1, an_all.at[rep])
        got(RAY + 3 + k - 1, an_all.at[rep])
    lane = lax.broadcasted_iota(jnp.int32, (16, 128), 1)

    def merge(r):
        sl = pl.ds(r, 16)
        for q in range(4):
            def put(lo, width, v):
                cols = pl.ds(q * 1152 + lo, width)
                ni_ref[0, sl, cols] = (0.5 * v + 0.5 * st[sl, cols].astype(F32)).astype(BF)

            even = an_all[2 * q, sl, :].astype(F32)
            odd = an_all[2 * q + 1, sl, :].astype(F32)
            put(0, 512, even[:, :512])
            put(512, 128, jnp.where(lane < 64, even[:, 512:], odd[:, :128]))
            put(640, 512, odd[:, 128:])

    strips(BLK, merge)

    for h in (0, 1):
        for k in (1, 2, 3):
            for zz in (0, 1):
                got(RRY + h * 6 + (k - 1) * 2 + zz, ry.at[k - 1, zz, rows(h)])

        def total(zz, sl):
            v = st[sl, pl.ds(piece(zz, y), WIDE)].astype(F32)
            for k in range(3):
                v = v + ry[k, zz, sl, :].astype(F32)
            return v

        def give(r, h=h):
            sl = pl.ds(h * H + r, 16)
            tz[sl, :] = total(1 - zl, sl).astype(BF)

        strips(H, give)
        go(RRZ + h, tz.at[rows(h)], rzl.at[rows(h)], lpeer)
    for h in (0, 1):
        got(RRZ + h, rzl.at[rows(h)])

        def finish(r, h=h):
            sl = pl.ds(h * H + r, 16)
            v = total(zl, sl) + rzl[sl, :].astype(F32)
            v = jnp.where((y % 2) == 1, pltpu.roll(v, PIECE, 1), v)
            og_ref[sl, :] = anchor_ref[sl, :] - v[:, :PIECE] * 0.125

        strips(H, finish)

    for slot in range(8):
        got(IG + slot, ig_own.at[slot])
    for cp in stores:
        cp.wait()
    for m in sent:
        m.wait_send()


def per_device(attn_out, grad_out, inner_w, anchor, momentum, delayed):
    tok, d = grad_out.shape
    hd = attn_out.shape[1]
    hbm = pl.BlockSpec(memory_space=pl.ANY)
    vm = pl.BlockSpec(memory_space=pltpu.VMEM)
    shape = jax.ShapeDtypeStruct
    return pl.pallas_call(
        kernel,
        out_shape=(
            shape((tok, hd), BF),
            shape(inner_w.shape, BF),
            shape(anchor.shape, F32),
            shape(anchor.shape, F32),
            shape(anchor.shape, F32),
        ),
        in_specs=[hbm, hbm, hbm, vm, vm, vm],
        out_specs=(hbm, vm, vm, vm, vm),
        scratch_shapes=[
            pltpu.VMEM((8, BLK, d), BF),
            pltpu.VMEM((2 * tok, d), BF),
            pltpu.VMEM((2 * tok, hd), BF),
            pltpu.VMEM((2 * BLK, 2 * tok), BF),
            pltpu.VMEM((4, 2, BLK, d), BF),
            pltpu.VMEM((2, 2, H, d), BF),
            pltpu.VMEM((2, 2, H, d), BF),
            pltpu.VMEM((2, 2, H, d), BF),
            pltpu.VMEM((2, H, d), BF),
            pltpu.VMEM((8, tok, BLK), BF),
            pltpu.VMEM((8, tok, BLK), BF),
            pltpu.VMEM((BLK, d), BF),
            pltpu.VMEM((8, BLK, WIDE), BF),
            pltpu.VMEM((3, 2, BLK, WIDE), BF),
            pltpu.VMEM((BLK, WIDE), BF),
            pltpu.VMEM((BLK, WIDE), BF),
            pltpu.VMEM((BLK, WIDE), F32),
            pltpu.SemaphoreType.DMA((N_MSG,)),
            pltpu.SemaphoreType.DMA((N_MSG,)),
            pltpu.SemaphoreType.DMA((11,)),
        ],
        compiler_params=pltpu.CompilerParams(
            collective_id=0, has_side_effects=True, vmem_limit_bytes=60 * 2**20
        ),
    )(attn_out, grad_out, inner_w, anchor, momentum, delayed)


def solution(mesh):
    return jax.shard_map(
        per_device,
        mesh=mesh,
        in_specs=(
            P(("rep", "fsdp"), None),
            P(("rep", "fsdp"), None),
            P("rep", "fsdp", None),
            P("fsdp", "rep"),
            P("fsdp", "rep"),
            P("fsdp", "rep"),
        ),
        out_specs=(
            P(("rep", "fsdp"), None),
            P("rep", "fsdp", None),
            P("fsdp", "rep"),
            P("fsdp", "rep"),
            P("fsdp", "rep"),
        ),
        check_vma=False,
    )
```

```python
import functools

import jax
import jax.numpy as jnp
from jax import lax
from jax.experimental import pallas as pl
from jax.experimental.pallas import tpu as pltpu
from jax.sharding import PartitionSpec as P

MESH = pl.DeviceIdType.MESH
BF = jnp.bfloat16
F32 = jnp.float32

BLK = 128
H = 64
NJ = 4
CR = BLK // NJ
HR = CR // 2
TILE_N = 1536
TILE_M = 512
PIECE = 576
WIDE = 640


def numbers(**counts):
    first, at = {}, 0
    for name, count in counts.items():
        first[name] = at
        at += count
    return first, at


FIRST, N_MSG = numbers(
    AGX=4, AGF=4, AGZ=8, AGY=2, RS1=4 * NJ, RSD=4 * NJ, RS2=4 * NJ, RSZ=NJ, SIBG=1, SIBA=1, IG=8,
    RAZ=1, RAY=6, RRY=6 * NJ, RRZ=NJ,
)


def kernel(
    a_hbm, g_hbm, w_hbm, anchor_ref, mom_ref, del_ref,
    ig_hbm, ni_ref, sum_ref,
    w_all, g_all, a_all, a_t, part, rx1, rxd, rx2, rxz,
    ig_own, ig_tx, st, an_all, ry, tz, rzl, total_ref, pad,
    send, recv, local,
):
    d = g_hbm.shape[1]
    tok = g_hbm.shape[0]
    factor = d ** (-0.5)
    rep = lax.axis_index("rep")
    fs = lax.axis_index("fsdp")
    x, zh, c = fs // 4, (fs // 2) % 2, fs % 2
    zl, y = rep // 4, rep % 4

    def at_x(k):
        return (x + k) % 4

    def fs_of(xx, zz, cc):
        return xx * 4 + zz * 2 + cc

    sib = (rep, fs_of(x, zh, 1 - c))
    zpeer = (rep, fs_of(x, 1 - zh, c))
    xpeer = {k: (rep, fs_of(at_x(k), zh, c)) for k in (1, 3)}
    ypeer = {k: (zl * 4 + (y + k) % 4, fs) for k in (1, 2, 3)}
    lpeer = ((1 - zl) * 4 + y, fs)

    def blk(k, zi):
        return at_x(k) * 2 + (zh if zi else 1 - zh)

    def msg(name, i, src, dst, dev):
        n = FIRST[name] + i
        return pltpu.make_async_remote_copy(
            src_ref=src, dst_ref=dst, send_sem=send.at[n], recv_sem=recv.at[n],
            device_id=dev, device_id_type=MESH,
        )

    sent = []

    def go(name, i, src, dst, dev):
        m = msg(name, i, src, dst, dev)
        m.start()
        sent.append(m)

    def got(name, i, ref):
        msg(name, i, ref, ref, sib).wait_recv()

    def half(h):
        return pl.ds(h * H, H)

    def quarter(h, part_of):
        return pl.ds(h * H + part_of * (H // 2), H // 2)

    def chunk(j):
        return pl.ds(j * CR, CR)

    def piece_rows(j, h):
        return pl.ds(j * CR + h * HR, HR)

    own = blk(0, 1)
    shift = pl.multiple_of((y % 2) * (WIDE - PIECE), WIDE - PIECE)

    load_g = pltpu.make_async_copy(g_hbm, g_all.at[pl.ds(0, tok)], local.at[0])
    load_a = pltpu.make_async_copy(a_hbm, a_all.at[pl.ds(0, tok)], local.at[1])
    load_w = pltpu.make_async_copy(w_hbm.at[0], w_all.at[own], local.at[2])

    barrier = pltpu.get_barrier_semaphore()
    peers = [sib, zpeer, xpeer[1], xpeer[3], ypeer[1], ypeer[2], ypeer[3], lpeer]
    for p in peers:
        pl.semaphore_signal(barrier, inc=1, device_id=p, device_id_type=MESH)
    load_g.start()
    load_a.start()
    load_w.start()
    pl.semaphore_wait(barrier, len(peers))

    go("SIBA", 0, a_hbm, a_all.at[pl.ds(tok, tok)], sib)
    go("SIBG", 0, g_hbm, g_all.at[pl.ds(tok, tok)], sib)
    for h in (0, 1):
        for way, k in ((0, 1), (1, 3)):
            hh = h if way == 0 else 1 - h
            go("AGX", way * 2 + hh, w_hbm.at[0, half(hh)], w_all.at[own, half(hh)], xpeer[k])
        go("AGZ", h, w_hbm.at[0, half(h)], w_all.at[own, half(h)], zpeer)

    pad[...] = jnp.zeros_like(pad)
    momentum = 0.9 * mom_ref[...] + del_ref[...]
    pad[pl.ds(shift, PIECE), :] = anchor_ref[...] - 0.7 * (del_ref[...] + 0.9 * momentum)
    an_all[rep] = pad[...].T.astype(BF)
    go("RAZ", 0, an_all.at[rep], an_all.at[rep], lpeer)
    for k in (1, 2, 3):
        go("RAY", k - 1, an_all.at[rep], an_all.at[rep], ypeer[k])

    load_a.wait()
    load_g.wait()
    got("SIBA", 0, a_hbm)
    got("SIBG", 0, g_hbm)

    def products(k):
        for zi in (0, 1):
            col = pl.multiple_of(fs_of(at_x(k), zh if zi else 1 - zh, c) * BLK, BLK)
            a_t[pl.ds(zi * BLK, BLK), :] = a_all[:, pl.ds(col, BLK)].T

        def step(n, carry):
            cols = pl.ds(pl.multiple_of(n * TILE_N, TILE_N), TILE_N)
            r = jnp.dot(a_t[...], g_all[:, cols], preferred_element_type=F32) * factor
            part[k, 0, :, cols] = r[:BLK].astype(BF)
            part[k, 1, :, cols] = r[BLK:].astype(BF)
            return carry

        lax.fori_loop(0, d // TILE_N, step, 0)

    def rs_id(zi, j, h):
        return (zi * NJ + j) * 2 + h

    def first(zi):
        for j in range(NJ):
            for h, k in ((0, 1), (1, 3)):
                go("RS1", rs_id(zi, j, h), part.at[2, zi, piece_rows(j, h)], rx1.at[zi, j, h], xpeer[k])

    def direct(zi, j):
        for h, k in ((1, 1), (0, 3)):
            go("RSD", rs_id(zi, j, h), part.at[k, zi, piece_rows(j, h)], rxd.at[zi, j, h], xpeer[k])

    def second(zi, j):
        for h, k in ((0, 1), (1, 3)):
            got("RS1", rs_id(zi, j, h), rx1.at[zi, j, h])
            sl = piece_rows(j, h)
            v = part[k, zi, sl, :].astype(F32) + rx1[zi, j, h].astype(F32)
            part[k, zi, sl, :] = v.astype(BF)
            go("RS2", rs_id(zi, j, h), part.at[k, zi, sl], rx2.at[zi, j, h], xpeer[k])

    stores = []

    def input_grad(slot, k, zi):
        b = blk(k, zi)

        def tile(r):
            return (
                lax.dot_general(
                    g_all[pl.ds(r, TILE_M), :], w_all[b], (((1,), (1,)), ((), ())),
                    preferred_element_type=F32,
                )
                * factor
            ).astype(BF)

        col = pl.multiple_of(fs_of(at_x(k), zh if zi else 1 - zh, c) * BLK, BLK)
        there = ig_hbm.at[:, pl.ds(col, BLK)]
        for r in range(0, tok, TILE_M):
            ig_tx[slot, pl.ds(r, TILE_M), :] = tile(tok + r)
        go("IG", slot, ig_tx.at[slot], there, sib)
        for r in range(0, tok, TILE_M):
            ig_own[slot, pl.ds(r, TILE_M), :] = tile(r)
        cp = pltpu.make_async_copy(ig_own.at[slot], there, local.at[3 + slot])
        cp.start()
        stores.append(cp)

    products(2)
    first(0)
    products(1)
    products(3)
    for j in range(NJ):
        direct(0, j)
    products(0)
    load_w.wait()

    for way, k in ((0, 3), (1, 1)):
        for h in (0, 1):
            ref = w_all.at[blk(k, 1), half(h)]
            got("AGX", way * 2 + h, ref)
            go("AGZ", 2 + way * 2 + h, ref, ref, zpeer)

    for j in range(NJ):
        second(0, j)
    first(1)

    def onward(part_of):
        for way, k in ((0, 3), (1, 1)):
            ref = w_all.at[blk(k, 1), quarter(way, part_of)]
            go("AGF", way * 2 + part_of, ref, ref, xpeer[1 if way == 0 else 3])

    onward(0)

    got("RAZ", 0, an_all.at[lpeer[0]])
    for k in (1, 2, 3):
        ref = an_all.at[lpeer[0]]
        go("RAY", 3 + k - 1, ref, ref, ypeer[k])

    input_grad(0, 0, 1)
    input_grad(1, 1, 1)
    input_grad(2, 3, 1)

    for j in range(NJ):
        for h in (0, 1):
            got("RSD", rs_id(0, j, h), rxd.at[0, j, h])
            got("RS2", rs_id(0, j, h), rx2.at[0, j, h])
            sl = piece_rows(j, h)
            v = part[0, 0, sl, :].astype(F32) + rxd[0, j, h].astype(F32) + rx2[0, j, h].astype(F32)
            part[0, 0, sl, :] = v.astype(BF)
        go("RSZ", j, part.at[0, 0, chunk(j)], rxz.at[j], zpeer)

    for j in range(NJ):
        direct(1, j)
        second(1, j)
    onward(1)

    for h in (0, 1):
        got("AGZ", h, w_all.at[blk(0, 0), half(h)])
    for way, k in ((0, 3), (1, 1)):
        for h in (0, 1):
            got("AGZ", 2 + way * 2 + h, w_all.at[blk(k, 0), half(h)])
        ref = w_all.at[blk(k, 0), quarter(way, 1)]
        go("AGY", way, ref, ref, xpeer[1 if way == 0 else 3])
    for h in (0, 1):
        ref = w_all.at[blk(2, 1), quarter(h, 0)]
        got("AGF", h * 2, ref)
        go("AGZ", 6 + h, ref, ref, zpeer)
    input_grad(3, 0, 0)
    input_grad(4, 1, 0)

    def piece(zz, yy):
        return pl.multiple_of(zz * 2304 + (yy // 2) * 1152 + (yy % 2) * 512, 128)

    def stepped(j):
        got("RSZ", j, rxz.at[j])
        for h in (0, 1):
            got("RSD", rs_id(1, j, h), rxd.at[1, j, h])
            got("RS2", rs_id(1, j, h), rx2.at[1, j, h])
            sl = piece_rows(j, h)
            v = (part[0, 1, sl, :].astype(F32) + rxd[1, j, h].astype(F32)) + (
                rx2[1, j, h].astype(F32) + rxz[j, pl.ds(h * HR, HR), :].astype(F32)
            )
            st[sl, :] = (w_all[own, sl, :].astype(F32) - v).astype(BF)
        for k in (1, 2, 3):
            for zz in (0, 1):
                col = piece(zz, (y + k) % 4)
                go(
                    "RRY", j * 6 + (k - 1) * 2 + zz,
                    st.at[chunk(j), pl.ds(col, WIDE)], ry.at[k - 1, zz, chunk(j)], ypeer[k],
                )

    def over_y(j):
        for k in (1, 2, 3):
            for zz in (0, 1):
                got("RRY", j * 6 + (k - 1) * 2 + zz, ry.at[k - 1, zz, chunk(j)])

        def total(zz):
            v = st[chunk(j), pl.ds(piece(zz, y), WIDE)].astype(F32)
            for k in range(3):
                v = v + ry[k, zz, chunk(j), :].astype(F32)
            return v

        tz[chunk(j), :] = total(1 - zl).astype(BF)
        go("RRZ", j, tz.at[chunk(j)], rzl.at[chunk(j)], lpeer)
        total_ref[chunk(j), :] = total(zl)

    for j in range(NJ):
        stepped(j)
        if j == 0:
            input_grad(5, 3, 0)
        else:
            over_y(j - 1)

    for k in (1, 2, 3):
        got("RAY", k - 1, an_all.at[rep])
        got("RAY", 3 + k - 1, an_all.at[rep])
    lane = lax.broadcasted_iota(jnp.int32, (16, 128), 1)

    def merge(i, carry):
        sl = pl.ds(pl.multiple_of(i * 16, 16), 16)
        for q in range(4):
            def put(lo, width, v):
                cols = pl.ds(q * 1152 + lo, width)
                ni_ref[0, sl, cols] = (0.5 * v + 0.5 * st[sl, cols].astype(F32)).astype(BF)

            even = an_all[2 * q, sl, :].astype(F32)
            odd = an_all[2 * q + 1, sl, :].astype(F32)
            put(0, 512, even[:, :512])
            put(512, 128, jnp.where(lane < 64, even[:, 512:], odd[:, :128]))
            put(640, 512, odd[:, 128:])
        return carry

    lax.fori_loop(0, BLK // 16, merge, 0)
    over_y(NJ - 1)

    for h in (0, 1):
        got("AGF", h * 2 + 1, w_all.at[blk(2, 1), quarter(h, 1)])
    input_grad(6, 2, 1)

    for j in range(NJ):
        got("RRZ", j, rzl.at[chunk(j)])
    pad[...] = (total_ref[...] + rzl[...].astype(F32)).T
    sum_ref[...] = pad[pl.ds(shift, PIECE), :]

    for h in (0, 1):
        got("AGZ", 6 + h, w_all.at[blk(2, 0), quarter(h, 0)])
        got("AGY", h, w_all.at[blk(2, 0), quarter(h, 1)])
    input_grad(7, 2, 0)

    for slot in range(8):
        got("IG", slot, ig_own.at[slot])
    for cp in stores:
        cp.wait()
    for m in sent:
        m.wait_send()


def per_device(attn_out, grad_out, inner_w, anchor, momentum, delayed):
    tok, d = grad_out.shape
    hd = attn_out.shape[1]
    hbm = pl.BlockSpec(memory_space=pl.ANY)
    vm = pl.BlockSpec(memory_space=pltpu.VMEM)
    shape = jax.ShapeDtypeStruct
    input_grad, new_inner, summed = pl.pallas_call(
        kernel,
        out_shape=(shape((tok, hd), BF), shape(inner_w.shape, BF), shape((PIECE, BLK), F32)),
        in_specs=[hbm, hbm, hbm, vm, vm, vm],
        out_specs=(hbm, vm, vm),
        scratch_shapes=[
            pltpu.VMEM((8, BLK, d), BF),
            pltpu.VMEM((2 * tok, d), BF),
            pltpu.VMEM((2 * tok, hd), BF),
            pltpu.VMEM((2 * BLK, 2 * tok), BF),
            pltpu.VMEM((4, 2, BLK, d), BF),
            pltpu.VMEM((2, NJ, 2, HR, d), BF),
            pltpu.VMEM((2, NJ, 2, HR, d), BF),
            pltpu.VMEM((2, NJ, 2, HR, d), BF),
            pltpu.VMEM((NJ, CR, d), BF),
            pltpu.VMEM((8, tok, BLK), BF),
            pltpu.VMEM((8, tok, BLK), BF),
            pltpu.VMEM((BLK, d), BF),
            pltpu.VMEM((8, BLK, WIDE), BF),
            pltpu.VMEM((3, 2, BLK, WIDE), BF),
            pltpu.VMEM((BLK, WIDE), BF),
            pltpu.VMEM((BLK, WIDE), BF),
            pltpu.VMEM((BLK, WIDE), F32),
            pltpu.VMEM((WIDE, BLK), F32),
            pltpu.SemaphoreType.DMA((N_MSG,)),
            pltpu.SemaphoreType.DMA((N_MSG,)),
            pltpu.SemaphoreType.DMA((11,)),
        ],
        compiler_params=pltpu.CompilerParams(
            collective_id=0, has_side_effects=True, vmem_limit_bytes=60 * 2**20
        ),
    )(attn_out, grad_out, inner_w, anchor.T, momentum.T, delayed.T)
    new_momentum = 0.9 * momentum + delayed
    new_anchor = anchor - 0.7 * (delayed + 0.9 * new_momentum)
    outer_grad = anchor - summed.T / lax.axis_size("rep")
    return (input_grad, new_inner, new_anchor, new_momentum, outer_grad)


def solution(mesh):
    return jax.shard_map(
        per_device,
        mesh=mesh,
        in_specs=(
            P(("rep", "fsdp"), None),
            P(("rep", "fsdp"), None),
            P("rep", "fsdp", None),
            P("fsdp", "rep"),
            P("fsdp", "rep"),
            P("fsdp", "rep"),
        ),
        out_specs=(
            P(("rep", "fsdp"), None),
            P("rep", "fsdp", None),
            P("fsdp", "rep"),
            P("fsdp", "rep"),
            P("fsdp", "rep"),
        ),
        check_vma=False,
    )
```

```python
import functools

import jax
import jax.numpy as jnp
from jax import lax
from jax.experimental import pallas as pl
from jax.experimental.pallas import tpu as pltpu
from jax.sharding import PartitionSpec as P

MESH = pl.DeviceIdType.MESH
BF = jnp.bfloat16
F32 = jnp.float32

BLK = 128
H = 64
NJ = 4
CR = BLK // NJ
HR = CR // 2
TILE_N = 1536
TILE_M = 512
NQ = 4
PIECE = 576
WIDE = 640


def numbers(**counts):
    first, at = {}, 0
    for name, count in counts.items():
        first[name] = at
        at += count
    return first, at


FIRST, N_MSG = numbers(
    AGX=4, AGF=4, AGZ=8, AGY=2 * NQ, RS1=4 * NJ, RSD=4 * NJ, RS2=4 * NJ, RSZ=NJ, SIBG=1, SIBA=1, IG=8,
    RAZ=1, RAY=6, RRY=6 * NJ, RRZ=NJ,
)


def kernel(
    a_hbm, g_hbm, w_hbm, anchor_hbm, mom_hbm, del_hbm,
    ig_hbm, ni_hbm, sum_hbm,
    w_all, g_all, a_all, a_t, part, rx1, rxd, rx2, rxz,
    ig_own, ig_tx, st, an_all, ry, tz, rzl, total_ref, pad,
    anchor_ref, mom_ref, del_ref, ni_ref, acc,
    send, recv, local,
):
    d = g_hbm.shape[1]
    tok = g_hbm.shape[0]
    factor = d ** (-0.5)
    rep = lax.axis_index("rep")
    fs = lax.axis_index("fsdp")
    x, zh, c = fs // 4, (fs // 2) % 2, fs % 2
    zl, y = rep // 4, rep % 4

    def at_x(k):
        return (x + k) % 4

    def fs_of(xx, zz, cc):
        return xx * 4 + zz * 2 + cc

    sib = (rep, fs_of(x, zh, 1 - c))
    zpeer = (rep, fs_of(x, 1 - zh, c))
    xpeer = {k: (rep, fs_of(at_x(k), zh, c)) for k in (1, 3)}
    ypeer = {k: (zl * 4 + (y + k) % 4, fs) for k in (1, 2, 3)}
    lpeer = ((1 - zl) * 4 + y, fs)

    def blk(k, zi):
        return at_x(k) * 2 + (zh if zi else 1 - zh)

    def msg(name, i, src, dst, dev):
        n = FIRST[name] + i
        return pltpu.make_async_remote_copy(
            src_ref=src, dst_ref=dst, send_sem=send.at[n], recv_sem=recv.at[n],
            device_id=dev, device_id_type=MESH,
        )

    sent, tail, early = [], [], []

    def go(name, i, src, dst, dev):
        m = msg(name, i, src, dst, dev)
        m.start()
        sent.append(m)
        if name == "AGY":
            tail.append(m)

    def got(name, i, ref):
        msg(name, i, ref, ref, sib).wait_recv()

    def half(h):
        return pl.ds(h * H, H)

    def quarter(h, part_of):
        return pl.ds(h * H + part_of * (H // 2), H // 2)

    def chunk(j):
        return pl.ds(j * CR, CR)

    def piece_rows(j, h):
        return pl.ds(j * CR + h * HR, HR)

    own = blk(0, 1)
    shift = pl.multiple_of((y % 2) * (WIDE - PIECE), WIDE - PIECE)

    load_g = pltpu.make_async_copy(g_hbm, g_all.at[pl.ds(0, tok)], local.at[0])
    load_a = pltpu.make_async_copy(a_hbm, a_all.at[pl.ds(0, tok)], local.at[1])
    load_w = pltpu.make_async_copy(w_hbm.at[0], w_all.at[own], local.at[2])

    small = [
        pltpu.make_async_copy(src, dst, local.at[11 + i])
        for i, (src, dst) in enumerate(
            ((anchor_hbm, anchor_ref), (mom_hbm, mom_ref), (del_hbm, del_ref))
        )
    ]

    barrier = pltpu.get_barrier_semaphore()
    peers = [sib, zpeer, xpeer[1], xpeer[3], ypeer[1], ypeer[2], ypeer[3], lpeer]
    for p in peers:
        pl.semaphore_signal(barrier, inc=1, device_id=p, device_id_type=MESH)
    for cp in small:
        cp.start()
    load_g.start()
    load_a.start()
    load_w.start()
    pl.semaphore_wait(barrier, len(peers))

    go("SIBA", 0, a_hbm, a_all.at[pl.ds(tok, tok)], sib)
    go("SIBG", 0, g_hbm, g_all.at[pl.ds(tok, tok)], sib)
    for h in (0, 1):
        for way, k in ((0, 1), (1, 3)):
            hh = h if way == 0 else 1 - h
            go("AGX", way * 2 + hh, w_hbm.at[0, half(hh)], w_all.at[own, half(hh)], xpeer[k])
        go("AGZ", h, w_hbm.at[0, half(h)], w_all.at[own, half(h)], zpeer)

    pad[...] = jnp.zeros_like(pad)
    for cp in small:
        cp.wait()
    momentum = 0.9 * mom_ref[...] + del_ref[...]
    pad[pl.ds(shift, PIECE), :] = anchor_ref[...] - 0.7 * (del_ref[...] + 0.9 * momentum)
    an_all[rep] = pad[...].T.astype(BF)
    go("RAZ", 0, an_all.at[rep], an_all.at[rep], lpeer)
    for k in (1, 2, 3):
        go("RAY", k - 1, an_all.at[rep], an_all.at[rep], ypeer[k])

    load_a.wait()
    load_g.wait()
    got("SIBA", 0, a_hbm)
    got("SIBG", 0, g_hbm)

    def products(k):
        for zi in (0, 1):
            col = pl.multiple_of(fs_of(at_x(k), zh if zi else 1 - zh, c) * BLK, BLK)
            a_t[pl.ds(zi * BLK, BLK), :] = a_all[:, pl.ds(col, BLK)].T

        def step(n, carry):
            cols = pl.ds(pl.multiple_of(n * TILE_N, TILE_N), TILE_N)
            r = jnp.dot(a_t[...], g_all[:, cols], preferred_element_type=F32) * factor
            part[k, 0, :, cols] = r[:BLK].astype(BF)
            part[k, 1, :, cols] = r[BLK:].astype(BF)
            return carry

        lax.fori_loop(0, d // TILE_N, step, 0)

    def rs_id(zi, j, h):
        return (zi * NJ + j) * 2 + h

    def first(zi):
        for j in range(NJ):
            for h, k in ((0, 1), (1, 3)):
                go("RS1", rs_id(zi, j, h), part.at[2, zi, piece_rows(j, h)], rx1.at[zi, j, h], xpeer[k])

    def direct(zi, j):
        for h, k in ((1, 1), (0, 3)):
            go("RSD", rs_id(zi, j, h), part.at[k, zi, piece_rows(j, h)], rxd.at[zi, j, h], xpeer[k])

    def second(zi, j):
        for h, k in ((0, 1), (1, 3)):
            got("RS1", rs_id(zi, j, h), rx1.at[zi, j, h])
            sl = piece_rows(j, h)
            v = part[k, zi, sl, :].astype(F32) + rx1[zi, j, h].astype(F32)
            part[k, zi, sl, :] = v.astype(BF)
            go("RS2", rs_id(zi, j, h), part.at[k, zi, sl], rx2.at[zi, j, h], xpeer[k])

    stores = []

    def input_grad(slot, k, zi):
        b = blk(k, zi)

        def tile(r):
            return (
                lax.dot_general(
                    g_all[pl.ds(r, TILE_M), :], w_all[b], (((1,), (1,)), ((), ())),
                    preferred_element_type=F32,
                )
                * factor
            ).astype(BF)

        col = pl.multiple_of(fs_of(at_x(k), zh if zi else 1 - zh, c) * BLK, BLK)
        there = ig_hbm.at[:, pl.ds(col, BLK)]
        for r in range(0, tok, TILE_M):
            ig_tx[slot, pl.ds(r, TILE_M), :] = tile(tok + r)
        go("IG", slot, ig_tx.at[slot], there, sib)
        for r in range(0, tok, TILE_M):
            ig_own[slot, pl.ds(r, TILE_M), :] = tile(r)
        cp = pltpu.make_async_copy(ig_own.at[slot], there, local.at[3 + slot])
        cp.start()
        stores.append(cp)

    def to_z(way, h):
        ref = w_all.at[blk(3 if way == 0 else 1, 1), half(h)]
        got("AGX", way * 2 + h, ref)
        go("AGZ", 2 + way * 2 + h, ref, ref, zpeer)

    products(2)
    first(0)
    products(1)
    to_z(0, 0)
    to_z(1, 1)
    products(3)
    for j in range(NJ):
        direct(0, j)
    products(0)
    load_w.wait()
    to_z(0, 1)
    to_z(1, 0)

    for j in range(NJ):
        second(0, j)
    first(1)

    def onward(part_of):
        for way, k in ((0, 3), (1, 1)):
            ref = w_all.at[blk(k, 1), quarter(way, part_of)]
            go("AGF", way * 2 + part_of, ref, ref, xpeer[1 if way == 0 else 3])

    onward(0)

    got("RAZ", 0, an_all.at[lpeer[0]])
    for k in (1, 2, 3):
        ref = an_all.at[lpeer[0]]
        go("RAY", 3 + k - 1, ref, ref, ypeer[k])

    input_grad(0, 0, 1)
    input_grad(1, 1, 1)
    input_grad(2, 3, 1)

    for j in range(NJ):
        for h in (0, 1):
            got("RSD", rs_id(0, j, h), rxd.at[0, j, h])
            got("RS2", rs_id(0, j, h), rx2.at[0, j, h])
            sl = piece_rows(j, h)
            v = part[0, 0, sl, :].astype(F32) + rxd[0, j, h].astype(F32) + rx2[0, j, h].astype(F32)
            part[0, 0, sl, :] = v.astype(BF)
        go("RSZ", j, part.at[0, 0, chunk(j)], rxz.at[j], zpeer)

    for j in range(NJ):
        direct(1, j)
        second(1, j)
    onward(1)

    for h in (0, 1):
        got("AGZ", h, w_all.at[blk(0, 0), half(h)])
    later = []
    for way, k in ((0, 3), (1, 1)):
        for h in (0, 1):
            got("AGZ", 2 + way * 2 + h, w_all.at[blk(k, 0), half(h)])
        later.append((way, blk(k, 0)))
    for q in range(NQ):
        for way, b in later:
            ref = w_all.at[b, quarter(way, 1), pl.ds(q * (d // NQ), d // NQ)]
            go("AGY", way * NQ + q, ref, ref, xpeer[1 if way == 0 else 3])
    for h in (0, 1):
        ref = w_all.at[blk(2, 1), quarter(h, 0)]
        got("AGF", h * 2, ref)
        go("AGZ", 6 + h, ref, ref, zpeer)
    input_grad(3, 0, 0)
    input_grad(4, 1, 0)

    def piece(zz, yy):
        return pl.multiple_of(zz * 2304 + (yy // 2) * 1152 + (yy % 2) * 512, 128)

    def stepped(j):
        got("RSZ", j, rxz.at[j])
        for h in (0, 1):
            got("RSD", rs_id(1, j, h), rxd.at[1, j, h])
            got("RS2", rs_id(1, j, h), rx2.at[1, j, h])
            sl = piece_rows(j, h)
            v = (part[0, 1, sl, :].astype(F32) + rxd[1, j, h].astype(F32)) + (
                rx2[1, j, h].astype(F32) + rxz[j, pl.ds(h * HR, HR), :].astype(F32)
            )
            st[sl, :] = (w_all[own, sl, :].astype(F32) - v).astype(BF)
        for k in (1, 2, 3):
            for zz in (0, 1):
                col = piece(zz, (y + k) % 4)
                go(
                    "RRY", j * 6 + (k - 1) * 2 + zz,
                    st.at[chunk(j), pl.ds(col, WIDE)], ry.at[k - 1, zz, chunk(j)], ypeer[k],
                )

    def over_y(j):
        for k in (1, 2, 3):
            for zz in (0, 1):
                got("RRY", j * 6 + (k - 1) * 2 + zz, ry.at[k - 1, zz, chunk(j)])

        def total(zz):
            v = st[chunk(j), pl.ds(piece(zz, y), WIDE)].astype(F32)
            for k in range(3):
                v = v + ry[k, zz, chunk(j), :].astype(F32)
            return v

        tz[chunk(j), :] = total(1 - zl).astype(BF)
        go("RRZ", j, tz.at[chunk(j)], rzl.at[chunk(j)], lpeer)
        total_ref[chunk(j), :] = total(zl)

    for j in range(NJ):
        stepped(j)
        if j == 0:
            input_grad(5, 3, 0)
        else:
            over_y(j - 1)

    for k in (1, 2, 3):
        got("RAY", k - 1, an_all.at[rep])
        got("RAY", 3 + k - 1, an_all.at[rep])
    lane = lax.broadcasted_iota(jnp.int32, (16, 128), 1)

    def merge(i, carry):
        sl = pl.ds(pl.multiple_of(i * 16, 16), 16)
        for q in range(4):
            def put(lo, width, v):
                cols = pl.ds(q * 1152 + lo, width)
                ni_ref[0, sl, cols] = (0.5 * v + 0.5 * st[sl, cols].astype(F32)).astype(BF)

            even = an_all[2 * q, sl, :].astype(F32)
            odd = an_all[2 * q + 1, sl, :].astype(F32)
            put(0, 512, even[:, :512])
            put(512, 128, jnp.where(lane < 64, even[:, 512:], odd[:, :128]))
            put(640, 512, odd[:, 128:])
        return carry

    lax.fori_loop(0, BLK // 16, merge, 0)
    merged = pltpu.make_async_copy(ni_ref, ni_hbm, local.at[14])
    merged.start()
    over_y(NJ - 1)

    for h in (0, 1):
        got("AGF", h * 2 + 1, w_all.at[blk(2, 1), quarter(h, 1)])
    input_grad(6, 2, 1)

    for j in range(NJ):
        got("RRZ", j, rzl.at[chunk(j)])
    pad[...] = (total_ref[...] + rzl[...].astype(F32)).T
    summed = pltpu.make_async_copy(pad.at[pl.ds(shift, PIECE)], sum_hbm, local.at[15])
    summed.start()

    for h in (0, 1):
        got("AGZ", 6 + h, w_all.at[blk(2, 0), quarter(h, 0)])
    last = blk(2, 0)
    early.extend(m for m in sent if not any(m is t for t in tail))
    for m in early:
        m.wait_send()
    col = pl.multiple_of(fs_of(at_x(2), 1 - zh, c) * BLK, BLK)
    there = ig_hbm.at[:, pl.ds(col, BLK)]
    for q in range(NQ):
        cols = pl.ds(q * (d // NQ), d // NQ)
        for way in (0, 1):
            got("AGY", way * NQ + q, w_all.at[last, quarter(way, 1), cols])
        for r in (1, 0):
            sl = pl.ds(r * tok, tok)
            v = lax.dot_general(
                g_all[sl, cols], w_all[last, :, cols], (((1,), (1,)), ((), ())),
                preferred_element_type=F32,
            )
            if q > 0:
                v = v + acc[sl, :]
            if q < NQ - 1:
                acc[sl, :] = v
            elif r:
                ig_tx[7] = (v * factor).astype(BF)
                go("IG", 7, ig_tx.at[7], there, sib)
            else:
                ig_own[7] = (v * factor).astype(BF)
    cp = pltpu.make_async_copy(ig_own.at[7], there, local.at[10])
    cp.start()
    stores.append(cp)

    for slot in range(8):
        got("IG", slot, ig_own.at[slot])
    for cp in stores + [merged, summed]:
        cp.wait()
    for m in sent[len(early) + len(tail):] + tail:
        m.wait_send()


def finish(
    ig, ni, total, anchor, mom, delayed, ig_out, ni_out, na_out, nm_out, og_out,
    ig_v, ni_v, total_v, anchor_v, mom_v, del_v, na_v, nm_v, og_v, sem,
):
    copy = pltpu.make_async_copy
    pieces = [(total, total_v), (anchor, anchor_v), (mom, mom_v), (delayed, del_v)]
    loads = [copy(a, b, sem.at[i]) for i, (a, b) in enumerate(pieces)]
    n = len(loads)
    out = []
    rows = ig.shape[0] // 4
    for i in range(4):
        sl = pl.ds(i * rows, rows)
        out.append((ig.at[sl], ig_v.at[sl], ig_out.at[sl]))
    for i in range(2):
        sl = pl.ds(i * H, H)
        out.append((ni.at[0, sl], ni_v.at[sl], ni_out.at[0, sl]))
    through = [
        (copy(a, b, sem.at[n + i]), copy(b, c, sem.at[n + len(out) + i]))
        for i, (a, b, c) in enumerate(out)
    ]
    for cp in loads:
        cp.start()
    for cp, _ in through:
        cp.start()
    for cp in loads:
        cp.wait()
    momentum = 0.9 * mom_v[...] + del_v[...]
    nm_v[...] = momentum
    na_v[...] = anchor_v[...] - 0.7 * (del_v[...] + 0.9 * momentum)
    og_v[...] = anchor_v[...] - total_v[...] * 0.125
    n += 2 * len(out)
    done = [
        copy(a, b, sem.at[n + i])
        for i, (a, b) in enumerate(((nm_v, nm_out), (na_v, na_out), (og_v, og_out)))
    ]
    for cp in done:
        cp.start()
    for first, second in through:
        first.wait()
        second.start()
    for cp in done:
        cp.wait()
    for _, second in through:
        second.wait()


def per_device(attn_out, grad_out, inner_w, anchor, momentum, delayed):
    tok, d = grad_out.shape
    hd = attn_out.shape[1]
    hbm = pl.BlockSpec(memory_space=pl.ANY)
    shape = jax.ShapeDtypeStruct
    across = (anchor.T, momentum.T, delayed.T)
    input_grad, new_inner, summed = pl.pallas_call(
        kernel,
        out_shape=(shape((tok, hd), BF), shape(inner_w.shape, BF), shape((PIECE, BLK), F32)),
        in_specs=[hbm] * 6,
        out_specs=(hbm,) * 3,
        scratch_shapes=[
            pltpu.VMEM((8, BLK, d), BF),
            pltpu.VMEM((2 * tok, d), BF),
            pltpu.VMEM((2 * tok, hd), BF),
            pltpu.VMEM((2 * BLK, 2 * tok), BF),
            pltpu.VMEM((4, 2, BLK, d), BF),
            pltpu.VMEM((2, NJ, 2, HR, d), BF),
            pltpu.VMEM((2, NJ, 2, HR, d), BF),
            pltpu.VMEM((2, NJ, 2, HR, d), BF),
            pltpu.VMEM((NJ, CR, d), BF),
            pltpu.VMEM((8, tok, BLK), BF),
            pltpu.VMEM((8, tok, BLK), BF),
            pltpu.VMEM((BLK, d), BF),
            pltpu.VMEM((8, BLK, WIDE), BF),
            pltpu.VMEM((3, 2, BLK, WIDE), BF),
            pltpu.VMEM((BLK, WIDE), BF),
            pltpu.VMEM((BLK, WIDE), BF),
            pltpu.VMEM((BLK, WIDE), F32),
            pltpu.VMEM((WIDE, BLK), F32),
            pltpu.VMEM((PIECE, BLK), F32),
            pltpu.VMEM((PIECE, BLK), F32),
            pltpu.VMEM((PIECE, BLK), F32),
            pltpu.VMEM((1, BLK, d), BF),
            pltpu.VMEM((2 * tok, BLK), F32),
            pltpu.SemaphoreType.DMA((N_MSG,)),
            pltpu.SemaphoreType.DMA((N_MSG,)),
            pltpu.SemaphoreType.DMA((16,)),
        ],
        compiler_params=pltpu.CompilerParams(
            collective_id=0, has_side_effects=True, vmem_limit_bytes=60 * 2**20
        ),
    )(attn_out, grad_out, inner_w, *across)
    f32 = shape((PIECE, BLK), F32)
    input_grad, new_inner, *rest = pl.pallas_call(
        finish,
        out_shape=(shape((tok, hd), BF), shape(inner_w.shape, BF), f32, f32, f32),
        in_specs=[hbm] * 6,
        out_specs=(hbm,) * 5,
        scratch_shapes=[pltpu.VMEM((tok, hd), BF), pltpu.VMEM((BLK, d), BF)]
        + [pltpu.VMEM((PIECE, BLK), F32)] * 7
        + [pltpu.SemaphoreType.DMA((19,))],
        compiler_params=pltpu.CompilerParams(vmem_limit_bytes=60 * 2**20),
    )(input_grad, new_inner, summed, *across)
    return (input_grad, new_inner, *(v.T for v in rest))


def solution(mesh):
    return jax.shard_map(
        per_device,
        mesh=mesh,
        in_specs=(
            P(("rep", "fsdp"), None),
            P(("rep", "fsdp"), None),
            P("rep", "fsdp", None),
            P("fsdp", "rep"),
            P("fsdp", "rep"),
            P("fsdp", "rep"),
        ),
        out_specs=(
            P(("rep", "fsdp"), None),
            P("rep", "fsdp", None),
            P("fsdp", "rep"),
            P("fsdp", "rep"),
            P("fsdp", "rep"),
        ),
        check_vma=False,
    )
```

```python
import functools

import jax
import jax.numpy as jnp
from jax import lax
from jax.experimental import pallas as pl
from jax.experimental.pallas import tpu as pltpu
from jax.sharding import PartitionSpec as P

MESH = pl.DeviceIdType.MESH
BF = jnp.bfloat16
F32 = jnp.float32

BLK = 128
H = 64
NJ = 4
CR = BLK // NJ
HR = CR // 2
TILE_N = 1536
TILE_M = 512
NQ = 4
PIECE = 576
WIDE = 640


def numbers(**counts):
    first, at = {}, 0
    for name, count in counts.items():
        first[name] = at
        at += count
    return first, at


FIRST, N_MSG = numbers(
    AGX=4, AGF=4, AGZ=8, AGY=2 * NQ, RS1=4 * NJ, RSD=4 * NJ, RS2=4 * NJ, RSZ=NJ, SIBG=1, SIBA=1, IG=8,
    RAZ=1, RAY=6, RRY=6 * NJ, RRZ=NJ,
)


def kernel(
    a_hbm, g_hbm, w_hbm, anchor_hbm, mom_hbm, del_hbm,
    ig_ref, ni_ref, sum_ref,
    w_all, g_all, a_all, a_t, part, rx1, rxd, rx2, rxz,
    ig_tx, st, an_all, ry, tz, rzl, total_ref, pad,
    anchor_ref, mom_ref, del_ref, acc,
    send, recv, local,
):
    d = g_hbm.shape[1]
    tok = g_hbm.shape[0]
    factor = d ** (-0.5)
    rep = lax.axis_index("rep")
    fs = lax.axis_index("fsdp")
    x, zh, c = fs // 4, (fs // 2) % 2, fs % 2
    zl, y = rep // 4, rep % 4

    def at_x(k):
        return (x + k) % 4

    def fs_of(xx, zz, cc):
        return xx * 4 + zz * 2 + cc

    sib = (rep, fs_of(x, zh, 1 - c))
    zpeer = (rep, fs_of(x, 1 - zh, c))
    xpeer = {k: (rep, fs_of(at_x(k), zh, c)) for k in (1, 3)}
    ypeer = {k: (zl * 4 + (y + k) % 4, fs) for k in (1, 2, 3)}
    lpeer = ((1 - zl) * 4 + y, fs)

    def blk(k, zi):
        return at_x(k) * 2 + (zh if zi else 1 - zh)

    def msg(name, i, src, dst, dev):
        n = FIRST[name] + i
        return pltpu.make_async_remote_copy(
            src_ref=src, dst_ref=dst, send_sem=send.at[n], recv_sem=recv.at[n],
            device_id=dev, device_id_type=MESH,
        )

    sent, tail, early = [], [], []

    def go(name, i, src, dst, dev):
        m = msg(name, i, src, dst, dev)
        m.start()
        sent.append(m)
        if name == "AGY":
            tail.append(m)

    def got(name, i, ref):
        msg(name, i, ref, ref, sib).wait_recv()

    def half(h):
        return pl.ds(h * H, H)

    def quarter(h, part_of):
        return pl.ds(h * H + part_of * (H // 2), H // 2)

    def chunk(j):
        return pl.ds(j * CR, CR)

    def piece_rows(j, h):
        return pl.ds(j * CR + h * HR, HR)

    own = blk(0, 1)
    shift = pl.multiple_of((y % 2) * (WIDE - PIECE), WIDE - PIECE)

    load_g = pltpu.make_async_copy(g_hbm, g_all.at[pl.ds(0, tok)], local.at[0])
    load_a = pltpu.make_async_copy(a_hbm, a_all.at[pl.ds(0, tok)], local.at[1])
    load_w = pltpu.make_async_copy(w_hbm.at[0], w_all.at[own], local.at[2])

    small = [
        pltpu.make_async_copy(src, dst, local.at[3 + i])
        for i, (src, dst) in enumerate(
            ((anchor_hbm, anchor_ref), (mom_hbm, mom_ref), (del_hbm, del_ref))
        )
    ]

    barrier = pltpu.get_barrier_semaphore()
    peers = [sib, zpeer, xpeer[1], xpeer[3], ypeer[1], ypeer[2], ypeer[3], lpeer]
    for p in peers:
        pl.semaphore_signal(barrier, inc=1, device_id=p, device_id_type=MESH)
    for cp in small:
        cp.start()
    load_g.start()
    load_a.start()
    load_w.start()
    pl.semaphore_wait(barrier, len(peers))

    go("SIBA", 0, a_hbm, a_all.at[pl.ds(tok, tok)], sib)
    go("SIBG", 0, g_hbm, g_all.at[pl.ds(tok, tok)], sib)
    for h in (0, 1):
        for way, k in ((0, 1), (1, 3)):
            hh = h if way == 0 else 1 - h
            go("AGX", way * 2 + hh, w_hbm.at[0, half(hh)], w_all.at[own, half(hh)], xpeer[k])
        go("AGZ", h, w_hbm.at[0, half(h)], w_all.at[own, half(h)], zpeer)

    pad[...] = jnp.zeros_like(pad)
    for cp in small:
        cp.wait()
    momentum = 0.9 * mom_ref[...] + del_ref[...]
    pad[pl.ds(shift, PIECE), :] = anchor_ref[...] - 0.7 * (del_ref[...] + 0.9 * momentum)
    an_all[rep] = pad[...].T.astype(BF)
    go("RAZ", 0, an_all.at[rep], an_all.at[rep], lpeer)
    for k in (1, 2, 3):
        go("RAY", k - 1, an_all.at[rep], an_all.at[rep], ypeer[k])

    load_a.wait()
    load_g.wait()
    got("SIBA", 0, a_hbm)
    got("SIBG", 0, g_hbm)

    def products(k):
        for zi in (0, 1):
            col = pl.multiple_of(fs_of(at_x(k), zh if zi else 1 - zh, c) * BLK, BLK)
            a_t[pl.ds(zi * BLK, BLK), :] = a_all[:, pl.ds(col, BLK)].T

        def step(n, carry):
            cols = pl.ds(pl.multiple_of(n * TILE_N, TILE_N), TILE_N)
            r = jnp.dot(a_t[...], g_all[:, cols], preferred_element_type=F32) * factor
            part[k, 0, :, cols] = r[:BLK].astype(BF)
            part[k, 1, :, cols] = r[BLK:].astype(BF)
            return carry

        lax.fori_loop(0, d // TILE_N, step, 0)

    def rs_id(zi, j, h):
        return (zi * NJ + j) * 2 + h

    def first(zi):
        for j in range(NJ):
            for h, k in ((0, 1), (1, 3)):
                go("RS1", rs_id(zi, j, h), part.at[2, zi, piece_rows(j, h)], rx1.at[zi, j, h], xpeer[k])

    def direct(zi, j):
        for h, k in ((1, 1), (0, 3)):
            go("RSD", rs_id(zi, j, h), part.at[k, zi, piece_rows(j, h)], rxd.at[zi, j, h], xpeer[k])

    def second(zi, j):
        for h, k in ((0, 1), (1, 3)):
            got("RS1", rs_id(zi, j, h), rx1.at[zi, j, h])
            sl = piece_rows(j, h)
            v = part[k, zi, sl, :].astype(F32) + rx1[zi, j, h].astype(F32)
            part[k, zi, sl, :] = v.astype(BF)
            go("RS2", rs_id(zi, j, h), part.at[k, zi, sl], rx2.at[zi, j, h], xpeer[k])

    def input_grad(slot, k, zi):
        b = blk(k, zi)

        def tile(r):
            return (
                lax.dot_general(
                    g_all[pl.ds(r, TILE_M), :], w_all[b], (((1,), (1,)), ((), ())),
                    preferred_element_type=F32,
                )
                * factor
            ).astype(BF)

        col = pl.multiple_of(fs_of(at_x(k), zh if zi else 1 - zh, c) * BLK, BLK)
        there = ig_ref.at[:, pl.ds(col, BLK)]
        for r in range(0, tok, TILE_M):
            ig_tx[slot, pl.ds(r, TILE_M), :] = tile(tok + r)
        go("IG", slot, ig_tx.at[slot], there, sib)
        for r in range(0, tok, TILE_M):
            ig_ref[pl.ds(r, TILE_M), pl.ds(col, BLK)] = tile(r)

    def to_z(way, h):
        ref = w_all.at[blk(3 if way == 0 else 1, 1), half(h)]
        got("AGX", way * 2 + h, ref)
        go("AGZ", 2 + way * 2 + h, ref, ref, zpeer)

    products(2)
    first(0)
    products(1)
    to_z(0, 0)
    to_z(1, 1)
    products(3)
    for j in range(NJ):
        direct(0, j)
    products(0)
    load_w.wait()
    to_z(0, 1)
    to_z(1, 0)

    for j in range(NJ):
        second(0, j)
    first(1)

    def onward(part_of):
        for way, k in ((0, 3), (1, 1)):
            ref = w_all.at[blk(k, 1), quarter(way, part_of)]
            go("AGF", way * 2 + part_of, ref, ref, xpeer[1 if way == 0 else 3])

    onward(0)

    got("RAZ", 0, an_all.at[lpeer[0]])
    for k in (1, 2, 3):
        ref = an_all.at[lpeer[0]]
        go("RAY", 3 + k - 1, ref, ref, ypeer[k])

    input_grad(0, 0, 1)
    input_grad(1, 1, 1)
    input_grad(2, 3, 1)

    for j in range(NJ):
        for h in (0, 1):
            got("RSD", rs_id(0, j, h), rxd.at[0, j, h])
            got("RS2", rs_id(0, j, h), rx2.at[0, j, h])
            sl = piece_rows(j, h)
            v = part[0, 0, sl, :].astype(F32) + rxd[0, j, h].astype(F32) + rx2[0, j, h].astype(F32)
            part[0, 0, sl, :] = v.astype(BF)
        go("RSZ", j, part.at[0, 0, chunk(j)], rxz.at[j], zpeer)

    for j in range(NJ):
        direct(1, j)
        second(1, j)
    onward(1)

    for h in (0, 1):
        got("AGZ", h, w_all.at[blk(0, 0), half(h)])
    later = []
    for way, k in ((0, 3), (1, 1)):
        for h in (0, 1):
            got("AGZ", 2 + way * 2 + h, w_all.at[blk(k, 0), half(h)])
        later.append((way, blk(k, 0)))
    for q in range(NQ):
        for way, b in later:
            ref = w_all.at[b, quarter(way, 1), pl.ds(q * (d // NQ), d // NQ)]
            go("AGY", way * NQ + q, ref, ref, xpeer[1 if way == 0 else 3])
    for h in (0, 1):
        ref = w_all.at[blk(2, 1), quarter(h, 0)]
        got("AGF", h * 2, ref)
        go("AGZ", 6 + h, ref, ref, zpeer)
    input_grad(3, 0, 0)
    input_grad(4, 1, 0)

    def piece(zz, yy):
        return pl.multiple_of(zz * 2304 + (yy // 2) * 1152 + (yy % 2) * 512, 128)

    def stepped(j):
        got("RSZ", j, rxz.at[j])
        for h in (0, 1):
            got("RSD", rs_id(1, j, h), rxd.at[1, j, h])
            got("RS2", rs_id(1, j, h), rx2.at[1, j, h])
            sl = piece_rows(j, h)
            v = (part[0, 1, sl, :].astype(F32) + rxd[1, j, h].astype(F32)) + (
                rx2[1, j, h].astype(F32) + rxz[j, pl.ds(h * HR, HR), :].astype(F32)
            )
            st[sl, :] = (w_all[own, sl, :].astype(F32) - v).astype(BF)
        for k in (1, 2, 3):
            for zz in (0, 1):
                col = piece(zz, (y + k) % 4)
                go(
                    "RRY", j * 6 + (k - 1) * 2 + zz,
                    st.at[chunk(j), pl.ds(col, WIDE)], ry.at[k - 1, zz, chunk(j)], ypeer[k],
                )

    def over_y(j):
        for k in (1, 2, 3):
            for zz in (0, 1):
                got("RRY", j * 6 + (k - 1) * 2 + zz, ry.at[k - 1, zz, chunk(j)])

        def total(zz):
            v = st[chunk(j), pl.ds(piece(zz, y), WIDE)].astype(F32)
            for k in range(3):
                v = v + ry[k, zz, chunk(j), :].astype(F32)
            return v

        tz[chunk(j), :] = total(1 - zl).astype(BF)
        go("RRZ", j, tz.at[chunk(j)], rzl.at[chunk(j)], lpeer)
        total_ref[chunk(j), :] = total(zl)

    for j in range(NJ):
        stepped(j)
        if j == 0:
            input_grad(5, 3, 0)
        else:
            over_y(j - 1)

    for k in (1, 2, 3):
        got("RAY", k - 1, an_all.at[rep])
        got("RAY", 3 + k - 1, an_all.at[rep])
    lane = lax.broadcasted_iota(jnp.int32, (16, 128), 1)

    def merge(i, carry):
        sl = pl.ds(pl.multiple_of(i * 16, 16), 16)
        for q in range(4):
            def put(lo, width, v):
                cols = pl.ds(q * 1152 + lo, width)
                ni_ref[0, sl, cols] = (0.5 * v + 0.5 * st[sl, cols].astype(F32)).astype(BF)

            even = an_all[2 * q, sl, :].astype(F32)
            odd = an_all[2 * q + 1, sl, :].astype(F32)
            put(0, 512, even[:, :512])
            put(512, 128, jnp.where(lane < 64, even[:, 512:], odd[:, :128]))
            put(640, 512, odd[:, 128:])
        return carry

    lax.fori_loop(0, BLK // 16, merge, 0)
    over_y(NJ - 1)

    for h in (0, 1):
        got("AGF", h * 2 + 1, w_all.at[blk(2, 1), quarter(h, 1)])
    input_grad(6, 2, 1)

    for j in range(NJ):
        got("RRZ", j, rzl.at[chunk(j)])
    pad[...] = (total_ref[...] + rzl[...].astype(F32)).T
    sum_ref[...] = pad[pl.ds(shift, PIECE), :]

    for h in (0, 1):
        got("AGZ", 6 + h, w_all.at[blk(2, 0), quarter(h, 0)])
    last = blk(2, 0)
    early.extend(m for m in sent if not any(m is t for t in tail))
    for m in early:
        m.wait_send()
    col = pl.multiple_of(fs_of(at_x(2), 1 - zh, c) * BLK, BLK)
    there = ig_ref.at[:, pl.ds(col, BLK)]
    for q in range(NQ):
        cols = pl.ds(q * (d // NQ), d // NQ)
        for way in (0, 1):
            got("AGY", way * NQ + q, w_all.at[last, quarter(way, 1), cols])
        for r in (1, 0):
            sl = pl.ds(r * tok, tok)
            v = lax.dot_general(
                g_all[sl, cols], w_all[last, :, cols], (((1,), (1,)), ((), ())),
                preferred_element_type=F32,
            )
            if q > 0:
                v = v + acc[sl, :]
            if q < NQ - 1:
                acc[sl, :] = v
            elif r:
                ig_tx[7] = (v * factor).astype(BF)
                go("IG", 7, ig_tx.at[7], there, sib)
            else:
                ig_ref[:, pl.ds(col, BLK)] = (v * factor).astype(BF)

    for slot in range(8):
        got("IG", slot, ig_tx.at[slot])
    for m in sent[len(early) + len(tail):] + tail:
        m.wait_send()


def finish(
    ig, ni, total, anchor, mom, delayed, ig_out, ni_out, na_out, nm_out, og_out,
    na_v, nm_v, og_v, sem,
):
    copies = [
        pltpu.make_async_copy(a, b, sem.at[i])
        for i, (a, b) in enumerate(
            ((ig, ig_out), (ni, ni_out), (nm_v, nm_out), (na_v, na_out), (og_v, og_out))
        )
    ]
    copies[0].start()
    copies[1].start()
    momentum = 0.9 * mom[...] + delayed[...]
    nm_v[...] = momentum
    copies[2].start()
    na_v[...] = anchor[...] - 0.7 * (delayed[...] + 0.9 * momentum)
    copies[3].start()
    og_v[...] = anchor[...] - total[...] * 0.125
    copies[4].start()
    for cp in copies:
        cp.wait()


def per_device(attn_out, grad_out, inner_w, anchor, momentum, delayed):
    tok, d = grad_out.shape
    hd = attn_out.shape[1]
    hbm = pl.BlockSpec(memory_space=pl.ANY)
    vm = pl.BlockSpec(memory_space=pltpu.VMEM)
    shape = jax.ShapeDtypeStruct
    across = (anchor.T, momentum.T, delayed.T)
    input_grad, new_inner, summed = pl.pallas_call(
        kernel,
        out_shape=(
            pltpu.VMEM((tok, hd), BF), pltpu.VMEM(inner_w.shape, BF), pltpu.VMEM((PIECE, BLK), F32)
        ),
        in_specs=[hbm] * 6,
        out_specs=(vm,) * 3,
        scratch_shapes=[
            pltpu.VMEM((8, BLK, d), BF),
            pltpu.VMEM((2 * tok, d), BF),
            pltpu.VMEM((2 * tok, hd), BF),
            pltpu.VMEM((2 * BLK, 2 * tok), BF),
            pltpu.VMEM((4, 2, BLK, d), BF),
            pltpu.VMEM((2, NJ, 2, HR, d), BF),
            pltpu.VMEM((2, NJ, 2, HR, d), BF),
            pltpu.VMEM((2, NJ, 2, HR, d), BF),
            pltpu.VMEM((NJ, CR, d), BF),
            pltpu.VMEM((8, tok, BLK), BF),
            pltpu.VMEM((BLK, d), BF),
            pltpu.VMEM((8, BLK, WIDE), BF),
            pltpu.VMEM((3, 2, BLK, WIDE), BF),
            pltpu.VMEM((BLK, WIDE), BF),
            pltpu.VMEM((BLK, WIDE), BF),
            pltpu.VMEM((BLK, WIDE), F32),
            pltpu.VMEM((WIDE, BLK), F32),
            pltpu.VMEM((PIECE, BLK), F32),
            pltpu.VMEM((PIECE, BLK), F32),
            pltpu.VMEM((PIECE, BLK), F32),
            pltpu.VMEM((2 * tok, BLK), F32),
            pltpu.SemaphoreType.DMA((N_MSG,)),
            pltpu.SemaphoreType.DMA((N_MSG,)),
            pltpu.SemaphoreType.DMA((6,)),
        ],
        compiler_params=pltpu.CompilerParams(
            collective_id=0, has_side_effects=True, vmem_limit_bytes=57 * 2**20
        ),
    )(attn_out, grad_out, inner_w, *across)
    f32 = shape((PIECE, BLK), F32)
    input_grad, new_inner, *rest = pl.pallas_call(
        finish,
        out_shape=(shape((tok, hd), BF), shape(inner_w.shape, BF), f32, f32, f32),
        in_specs=[vm] * 6,
        out_specs=(hbm,) * 5,
        scratch_shapes=[pltpu.VMEM((PIECE, BLK), F32)] * 3 + [pltpu.SemaphoreType.DMA((5,))],
        compiler_params=pltpu.CompilerParams(vmem_limit_bytes=16 * 2**20),
    )(input_grad, new_inner, summed, *across)
    return (input_grad, new_inner, *(v.T for v in rest))


def solution(mesh):
    return jax.shard_map(
        per_device,
        mesh=mesh,
        in_specs=(
            P(("rep", "fsdp"), None),
            P(("rep", "fsdp"), None),
            P("rep", "fsdp", None),
            P("fsdp", "rep"),
            P("fsdp", "rep"),
            P("fsdp", "rep"),
        ),
        out_specs=(
            P(("rep", "fsdp"), None),
            P("rep", "fsdp", None),
            P("fsdp", "rep"),
            P("fsdp", "rep"),
            P("fsdp", "rep"),
        ),
        check_vma=False,
    )
```

```python
import functools

import jax
import jax.numpy as jnp
from jax import lax
from jax.experimental import pallas as pl
from jax.experimental.pallas import tpu as pltpu
from jax.sharding import PartitionSpec as P

MESH = pl.DeviceIdType.MESH
BF = jnp.bfloat16
F32 = jnp.float32

BLK = 128
H = 64
NJ = 4
CR = BLK // NJ
HR = CR // 2
TILE_N = 1536
TILE_M = 512
NQ = 4
PIECE = 576
WIDE = 640


def numbers(**counts):
    first, at = {}, 0
    for name, count in counts.items():
        first[name] = at
        at += count
    return first, at


FIRST, N_MSG = numbers(
    AGX=4, AGF=4, AGZ=8, AGY=2 * NQ, RS1=4 * NJ, RSD=4 * NJ, RS2=4 * NJ, RSZ=NJ, SIBG=1, SIBA=1, IG=8,
    RAZ=1, RAY=6, RRY=6 * NJ, RRZ=NJ,
)


def kernel(
    a_hbm, g_hbm, w_hbm, anchor_hbm, mom_hbm, del_hbm,
    ig_ref, ni_ref, sum_ref,
    w_all, g_all, a_all, a_t, part, rx1, rxd, rx2, rxz,
    ig_tx, st, an_all, ry, tz, rzl, total_ref, pad,
    anchor_ref, mom_ref, del_ref, acc,
    send, recv, local,
):
    d = g_hbm.shape[1]
    tok = g_hbm.shape[0]
    factor = d ** (-0.5)
    rep = lax.axis_index("rep")
    fs = lax.axis_index("fsdp")
    x, zh, c = fs // 4, (fs // 2) % 2, fs % 2
    zl, y = rep // 4, rep % 4

    def at_x(k):
        return (x + k) % 4

    def fs_of(xx, zz, cc):
        return xx * 4 + zz * 2 + cc

    sib = (rep, fs_of(x, zh, 1 - c))
    zpeer = (rep, fs_of(x, 1 - zh, c))
    xpeer = {k: (rep, fs_of(at_x(k), zh, c)) for k in (1, 3)}
    ypeer = {k: (zl * 4 + (y + k) % 4, fs) for k in (1, 2, 3)}
    lpeer = ((1 - zl) * 4 + y, fs)

    def blk(k, zi):
        return at_x(k) * 2 + (zh if zi else 1 - zh)

    def msg(name, i, src, dst, dev):
        n = FIRST[name] + i
        return pltpu.make_async_remote_copy(
            src_ref=src, dst_ref=dst, send_sem=send.at[n], recv_sem=recv.at[n],
            device_id=dev, device_id_type=MESH,
        )

    sent, late = [], []

    def rs_id(zi, j, h):
        return (zi * NJ + j) * 2 + h

    def go(name, i, src, dst, dev):
        m = msg(name, i, src, dst, dev)
        m.start()
        last = (
            name in ("AGY", "RRZ")
            or (name == "AGZ" and i >= 6)
            or (name == "AGF" and i % 2 == 1)
            or (name == "RRY" and i >= 6 * (NJ - 1))
            or (name in ("RSD", "RS2") and i >= rs_id(1, NJ - 1, 0))
            or (name == "IG" and i >= 5)
        )
        (late if last else sent).append(m)

    def got(name, i, ref):
        msg(name, i, ref, ref, sib).wait_recv()

    def half(h):
        return pl.ds(h * H, H)

    def quarter(h, part_of):
        return pl.ds(h * H + part_of * (H // 2), H // 2)

    def chunk(j):
        return pl.ds(j * CR, CR)

    def piece_rows(j, h):
        return pl.ds(j * CR + h * HR, HR)

    own = blk(0, 1)
    shift = pl.multiple_of((y % 2) * (WIDE - PIECE), WIDE - PIECE)

    load_g = pltpu.make_async_copy(g_hbm, g_all.at[pl.ds(0, tok)], local.at[0])
    load_a = pltpu.make_async_copy(a_hbm, a_all.at[pl.ds(0, tok)], local.at[1])
    load_w = pltpu.make_async_copy(w_hbm.at[0], w_all.at[own], local.at[2])

    small = [
        pltpu.make_async_copy(src, dst, local.at[3 + i])
        for i, (src, dst) in enumerate(
            ((anchor_hbm, anchor_ref), (mom_hbm, mom_ref), (del_hbm, del_ref))
        )
    ]

    barrier = pltpu.get_barrier_semaphore()
    peers = [sib, zpeer, xpeer[1], xpeer[3], ypeer[1], ypeer[2], ypeer[3], lpeer]
    for p in peers:
        pl.semaphore_signal(barrier, inc=1, device_id=p, device_id_type=MESH)
    for cp in small:
        cp.start()
    load_g.start()
    load_a.start()
    load_w.start()
    pl.semaphore_wait(barrier, len(peers))

    go("SIBA", 0, a_hbm, a_all.at[pl.ds(tok, tok)], sib)
    go("SIBG", 0, g_hbm, g_all.at[pl.ds(tok, tok)], sib)
    for h in (0, 1):
        for way, k in ((0, 1), (1, 3)):
            hh = h if way == 0 else 1 - h
            go("AGX", way * 2 + hh, w_hbm.at[0, half(hh)], w_all.at[own, half(hh)], xpeer[k])
        go("AGZ", h, w_hbm.at[0, half(h)], w_all.at[own, half(h)], zpeer)

    pad[...] = jnp.zeros_like(pad)
    for cp in small:
        cp.wait()
    momentum = 0.9 * mom_ref[...] + del_ref[...]
    pad[pl.ds(shift, PIECE), :] = anchor_ref[...] - 0.7 * (del_ref[...] + 0.9 * momentum)
    an_all[rep] = pad[...].T.astype(BF)
    go("RAZ", 0, an_all.at[rep], an_all.at[rep], lpeer)
    for k in (1, 2, 3):
        go("RAY", k - 1, an_all.at[rep], an_all.at[rep], ypeer[k])

    load_a.wait()
    load_g.wait()
    got("SIBA", 0, a_hbm)
    got("SIBG", 0, g_hbm)

    def products(k):
        for zi in (0, 1):
            col = pl.multiple_of(fs_of(at_x(k), zh if zi else 1 - zh, c) * BLK, BLK)
            a_t[pl.ds(zi * BLK, BLK), :] = a_all[:, pl.ds(col, BLK)].T

        def step(n, carry):
            cols = pl.ds(pl.multiple_of(n * TILE_N, TILE_N), TILE_N)
            r = jnp.dot(a_t[...], g_all[:, cols], preferred_element_type=F32) * factor
            part[k, 0, :, cols] = r[:BLK].astype(BF)
            part[k, 1, :, cols] = r[BLK:].astype(BF)
            return carry

        lax.fori_loop(0, d // TILE_N, step, 0)

    def first(zi):
        for j in range(NJ):
            for h, k in ((0, 1), (1, 3)):
                go("RS1", rs_id(zi, j, h), part.at[2, zi, piece_rows(j, h)], rx1.at[zi, j, h], xpeer[k])

    def direct(zi, j):
        for h, k in ((1, 1), (0, 3)):
            go("RSD", rs_id(zi, j, h), part.at[k, zi, piece_rows(j, h)], rxd.at[zi, j, h], xpeer[k])

    def second(zi, j):
        for h, k in ((0, 1), (1, 3)):
            got("RS1", rs_id(zi, j, h), rx1.at[zi, j, h])
            sl = piece_rows(j, h)
            v = part[k, zi, sl, :].astype(F32) + rx1[zi, j, h].astype(F32)
            part[k, zi, sl, :] = v.astype(BF)
            go("RS2", rs_id(zi, j, h), part.at[k, zi, sl], rx2.at[zi, j, h], xpeer[k])

    def input_grad(slot, k, zi):
        b = blk(k, zi)

        def tile(r):
            return (
                lax.dot_general(
                    g_all[pl.ds(r, TILE_M), :], w_all[b], (((1,), (1,)), ((), ())),
                    preferred_element_type=F32,
                )
                * factor
            ).astype(BF)

        col = pl.multiple_of(fs_of(at_x(k), zh if zi else 1 - zh, c) * BLK, BLK)
        there = ig_ref.at[:, pl.ds(col, BLK)]
        for r in range(0, tok, TILE_M):
            ig_tx[slot, pl.ds(r, TILE_M), :] = tile(tok + r)
        go("IG", slot, ig_tx.at[slot], there, sib)
        for r in range(0, tok, TILE_M):
            ig_ref[pl.ds(r, TILE_M), pl.ds(col, BLK)] = tile(r)

    def to_z(way, h):
        ref = w_all.at[blk(3 if way == 0 else 1, 1), half(h)]
        got("AGX", way * 2 + h, ref)
        go("AGZ", 2 + way * 2 + h, ref, ref, zpeer)

    products(2)
    first(0)
    products(1)
    to_z(0, 0)
    to_z(1, 1)
    products(3)
    for j in range(NJ):
        direct(0, j)
    products(0)
    load_w.wait()
    to_z(0, 1)
    to_z(1, 0)

    for j in range(NJ):
        second(0, j)
    first(1)

    def onward(part_of):
        for way, k in ((0, 3), (1, 1)):
            ref = w_all.at[blk(k, 1), quarter(way, part_of)]
            go("AGF", way * 2 + part_of, ref, ref, xpeer[1 if way == 0 else 3])

    onward(0)

    got("RAZ", 0, an_all.at[lpeer[0]])
    for k in (1, 2, 3):
        ref = an_all.at[lpeer[0]]
        go("RAY", 3 + k - 1, ref, ref, ypeer[k])

    input_grad(0, 0, 1)
    input_grad(1, 1, 1)
    input_grad(2, 3, 1)

    for j in range(NJ):
        for h in (0, 1):
            got("RSD", rs_id(0, j, h), rxd.at[0, j, h])
            got("RS2", rs_id(0, j, h), rx2.at[0, j, h])
            sl = piece_rows(j, h)
            v = part[0, 0, sl, :].astype(F32) + rxd[0, j, h].astype(F32) + rx2[0, j, h].astype(F32)
            part[0, 0, sl, :] = v.astype(BF)
        go("RSZ", j, part.at[0, 0, chunk(j)], rxz.at[j], zpeer)

    for j in range(NJ):
        direct(1, j)
        second(1, j)
    onward(1)

    for h in (0, 1):
        got("AGZ", h, w_all.at[blk(0, 0), half(h)])
    later = []
    for way, k in ((0, 3), (1, 1)):
        for h in (0, 1):
            got("AGZ", 2 + way * 2 + h, w_all.at[blk(k, 0), half(h)])
        later.append((way, blk(k, 0)))
    for q in range(NQ):
        for way, b in later:
            ref = w_all.at[b, quarter(way, 1), pl.ds(q * (d // NQ), d // NQ)]
            go("AGY", way * NQ + q, ref, ref, xpeer[1 if way == 0 else 3])
    for h in (0, 1):
        ref = w_all.at[blk(2, 1), quarter(h, 0)]
        got("AGF", h * 2, ref)
        go("AGZ", 6 + h, ref, ref, zpeer)
    input_grad(3, 0, 0)
    input_grad(4, 1, 0)

    def piece(zz, yy):
        return pl.multiple_of(zz * 2304 + (yy // 2) * 1152 + (yy % 2) * 512, 128)

    def stepped(j):
        got("RSZ", j, rxz.at[j])
        for h in (0, 1):
            got("RSD", rs_id(1, j, h), rxd.at[1, j, h])
            got("RS2", rs_id(1, j, h), rx2.at[1, j, h])
            sl = piece_rows(j, h)
            v = (part[0, 1, sl, :].astype(F32) + rxd[1, j, h].astype(F32)) + (
                rx2[1, j, h].astype(F32) + rxz[j, pl.ds(h * HR, HR), :].astype(F32)
            )
            st[sl, :] = (w_all[own, sl, :].astype(F32) - v).astype(BF)
        for k in (1, 2, 3):
            for zz in (0, 1):
                col = piece(zz, (y + k) % 4)
                go(
                    "RRY", j * 6 + (k - 1) * 2 + zz,
                    st.at[chunk(j), pl.ds(col, WIDE)], ry.at[k - 1, zz, chunk(j)], ypeer[k],
                )

    def over_y(j):
        for k in (1, 2, 3):
            for zz in (0, 1):
                got("RRY", j * 6 + (k - 1) * 2 + zz, ry.at[k - 1, zz, chunk(j)])

        def total(zz):
            v = st[chunk(j), pl.ds(piece(zz, y), WIDE)].astype(F32)
            for k in range(3):
                v = v + ry[k, zz, chunk(j), :].astype(F32)
            return v

        tz[chunk(j), :] = total(1 - zl).astype(BF)
        go("RRZ", j, tz.at[chunk(j)], rzl.at[chunk(j)], lpeer)
        total_ref[chunk(j), :] = total(zl)

    for j in range(NJ):
        stepped(j)
        if j == 0:
            input_grad(5, 3, 0)
        else:
            over_y(j - 1)

    for k in (1, 2, 3):
        got("RAY", k - 1, an_all.at[rep])
        got("RAY", 3 + k - 1, an_all.at[rep])
    lane = lax.broadcasted_iota(jnp.int32, (16, 128), 1)

    def merge(i, carry):
        sl = pl.ds(pl.multiple_of(i * 16, 16), 16)
        for q in range(4):
            def put(lo, width, v):
                cols = pl.ds(q * 1152 + lo, width)
                ni_ref[0, sl, cols] = (0.5 * v + 0.5 * st[sl, cols].astype(F32)).astype(BF)

            even = an_all[2 * q, sl, :].astype(F32)
            odd = an_all[2 * q + 1, sl, :].astype(F32)
            put(0, 512, even[:, :512])
            put(512, 128, jnp.where(lane < 64, even[:, 512:], odd[:, :128]))
            put(640, 512, odd[:, 128:])
        return carry

    lax.fori_loop(0, BLK // 16, merge, 0)
    for m in sent:
        m.wait_send()
    over_y(NJ - 1)

    for h in (0, 1):
        got("AGF", h * 2 + 1, w_all.at[blk(2, 1), quarter(h, 1)])
    input_grad(6, 2, 1)

    for h in (0, 1):
        got("AGZ", 6 + h, w_all.at[blk(2, 0), quarter(h, 0)])
    last = blk(2, 0)
    col = pl.multiple_of(fs_of(at_x(2), 1 - zh, c) * BLK, BLK)
    there = ig_ref.at[:, pl.ds(col, BLK)]
    for q in range(NQ):
        cols = pl.ds(q * (d // NQ), d // NQ)
        for way in (0, 1):
            got("AGY", way * NQ + q, w_all.at[last, quarter(way, 1), cols])
        for r in (1, 0):
            sl = pl.ds(r * tok, tok)
            v = lax.dot_general(
                g_all[sl, cols], w_all[last, :, cols], (((1,), (1,)), ((), ())),
                preferred_element_type=F32,
            )
            if q > 0:
                v = v + acc[sl, :]
            if q < NQ - 1:
                acc[sl, :] = v
            elif r:
                ig_tx[7] = (v * factor).astype(BF)
                go("IG", 7, ig_tx.at[7], there, sib)
            else:
                ig_ref[:, pl.ds(col, BLK)] = (v * factor).astype(BF)

    for j in range(NJ):
        got("RRZ", j, rzl.at[chunk(j)])
    pad[...] = (total_ref[...] + rzl[...].astype(F32)).T
    sum_ref[...] = pad[pl.ds(shift, PIECE), :]

    for slot in range(8):
        got("IG", slot, ig_tx.at[slot])
    for m in late:
        m.wait_send()


def finish(
    ig, ni, total, anchor, mom, delayed, ig_out, ni_out, na_out, nm_out, og_out,
    na_v, nm_v, og_v, sem,
):
    copies = [
        pltpu.make_async_copy(a, b, sem.at[i])
        for i, (a, b) in enumerate(
            ((ig, ig_out), (ni, ni_out), (nm_v, nm_out), (na_v, na_out), (og_v, og_out))
        )
    ]
    copies[0].start()
    copies[1].start()
    momentum = 0.9 * mom[...] + delayed[...]
    nm_v[...] = momentum
    copies[2].start()
    na_v[...] = anchor[...] - 0.7 * (delayed[...] + 0.9 * momentum)
    copies[3].start()
    og_v[...] = anchor[...] - total[...] * 0.125
    copies[4].start()
    for cp in copies:
        cp.wait()


def per_device(attn_out, grad_out, inner_w, anchor, momentum, delayed):
    tok, d = grad_out.shape
    hd = attn_out.shape[1]
    hbm = pl.BlockSpec(memory_space=pl.ANY)
    vm = pl.BlockSpec(memory_space=pltpu.VMEM)
    shape = jax.ShapeDtypeStruct
    across = (anchor.T, momentum.T, delayed.T)
    input_grad, new_inner, summed = pl.pallas_call(
        kernel,
        out_shape=(
            pltpu.VMEM((tok, hd), BF), pltpu.VMEM(inner_w.shape, BF), pltpu.VMEM((PIECE, BLK), F32)
        ),
        in_specs=[hbm] * 6,
        out_specs=(vm,) * 3,
        scratch_shapes=[
            pltpu.VMEM((8, BLK, d), BF),
            pltpu.VMEM((2 * tok, d), BF),
            pltpu.VMEM((2 * tok, hd), BF),
            pltpu.VMEM((2 * BLK, 2 * tok), BF),
            pltpu.VMEM((4, 2, BLK, d), BF),
            pltpu.VMEM((2, NJ, 2, HR, d), BF),
            pltpu.VMEM((2, NJ, 2, HR, d), BF),
            pltpu.VMEM((2, NJ, 2, HR, d), BF),
            pltpu.VMEM((NJ, CR, d), BF),
            pltpu.VMEM((8, tok, BLK), BF),
            pltpu.VMEM((BLK, d), BF),
            pltpu.VMEM((8, BLK, WIDE), BF),
            pltpu.VMEM((3, 2, BLK, WIDE), BF),
            pltpu.VMEM((BLK, WIDE), BF),
            pltpu.VMEM((BLK, WIDE), BF),
            pltpu.VMEM((BLK, WIDE), F32),
            pltpu.VMEM((WIDE, BLK), F32),
            pltpu.VMEM((PIECE, BLK), F32),
            pltpu.VMEM((PIECE, BLK), F32),
            pltpu.VMEM((PIECE, BLK), F32),
            pltpu.VMEM((2 * tok, BLK), F32),
            pltpu.SemaphoreType.DMA((N_MSG,)),
            pltpu.SemaphoreType.DMA((N_MSG,)),
            pltpu.SemaphoreType.DMA((6,)),
        ],
        compiler_params=pltpu.CompilerParams(
            collective_id=0, has_side_effects=True, vmem_limit_bytes=57 * 2**20
        ),
    )(attn_out, grad_out, inner_w, *across)
    f32 = shape((PIECE, BLK), F32)
    input_grad, new_inner, *rest = pl.pallas_call(
        finish,
        out_shape=(shape((tok, hd), BF), shape(inner_w.shape, BF), f32, f32, f32),
        in_specs=[vm] * 6,
        out_specs=(hbm,) * 5,
        scratch_shapes=[pltpu.VMEM((PIECE, BLK), F32)] * 3 + [pltpu.SemaphoreType.DMA((5,))],
        compiler_params=pltpu.CompilerParams(vmem_limit_bytes=16 * 2**20),
    )(input_grad, new_inner, summed, *across)
    return (input_grad, new_inner, *(v.T for v in rest))


def solution(mesh):
    return jax.shard_map(
        per_device,
        mesh=mesh,
        in_specs=(
            P(("rep", "fsdp"), None),
            P(("rep", "fsdp"), None),
            P("rep", "fsdp", None),
            P("fsdp", "rep"),
            P("fsdp", "rep"),
            P("fsdp", "rep"),
        ),
        out_specs=(
            P(("rep", "fsdp"), None),
            P("rep", "fsdp", None),
            P("fsdp", "rep"),
            P("fsdp", "rep"),
            P("fsdp", "rep"),
        ),
        check_vma=False,
    )
```

```python
import functools

import jax
import jax.numpy as jnp
from jax import lax
from jax.experimental import pallas as pl
from jax.experimental.pallas import tpu as pltpu
from jax.sharding import PartitionSpec as P

MESH = pl.DeviceIdType.MESH
BF = jnp.bfloat16
F32 = jnp.float32

BLK = 128
H = 64
NJ = 4
CR = BLK // NJ
HR = CR // 2
TILE_N = 1536
TILE_M = 512
NQ = 4
PIECE = 576
WIDE = 640


def numbers(**counts):
    first, at = {}, 0
    for name, count in counts.items():
        first[name] = at
        at += count
    return first, at


FIRST, N_MSG = numbers(
    AGX=4, AGF=4, AGZ=8, AGY=2 * NQ, RS1=4 * NJ, RSD=4 * NJ, RS2=4 * NJ, RSZ=NJ, SIBG=1, SIBA=1, IG=8,
    RAZ=1, RAY=6, RRY=6 * NJ, RRZ=NJ,
)


def kernel(
    a_hbm, g_hbm, w_hbm, anchor_hbm, mom_hbm, del_hbm,
    ig_ref, ni_ref, sum_ref,
    w_all, g_all, a_all, a_t, part, rx1, rxd, rx2, rxz,
    ig_tx, st, an_all, ry, tz, rzl, total_ref, pad,
    anchor_ref, mom_ref, del_ref, acc,
    send, recv, local,
):
    d = g_hbm.shape[1]
    tok = g_hbm.shape[0]
    factor = d ** (-0.5)
    rep = lax.axis_index("rep")
    fs = lax.axis_index("fsdp")
    x, zh, c = fs // 4, (fs // 2) % 2, fs % 2
    zl, y = rep // 4, rep % 4

    def at_x(k):
        return (x + k) % 4

    def fs_of(xx, zz, cc):
        return xx * 4 + zz * 2 + cc

    sib = (rep, fs_of(x, zh, 1 - c))
    zpeer = (rep, fs_of(x, 1 - zh, c))
    xpeer = {k: (rep, fs_of(at_x(k), zh, c)) for k in (1, 3)}
    ypeer = {k: (zl * 4 + (y + k) % 4, fs) for k in (1, 2, 3)}
    lpeer = ((1 - zl) * 4 + y, fs)

    def blk(k, zi):
        return at_x(k) * 2 + (zh if zi else 1 - zh)

    def msg(name, i, src, dst, dev):
        n = FIRST[name] + i
        return pltpu.make_async_remote_copy(
            src_ref=src, dst_ref=dst, send_sem=send.at[n], recv_sem=recv.at[n],
            device_id=dev, device_id_type=MESH,
        )

    sent, late = [], []

    def rs_id(zi, j, h):
        return (zi * NJ + j) * 2 + h

    def go(name, i, src, dst, dev):
        m = msg(name, i, src, dst, dev)
        m.start()
        last = (
            name in ("AGY", "RRZ")
            or (name == "AGZ" and i >= 6)
            or (name == "AGF" and i % 2 == 1)
            or (name == "RRY" and i >= 6 * (NJ - 1))
            or (name in ("RSD", "RS2") and i >= rs_id(1, NJ - 1, 0))
            or (name == "IG" and i >= 5)
        )
        (late if last else sent).append(m)

    def got(name, i, ref):
        msg(name, i, ref, ref, sib).wait_recv()

    def half(h):
        return pl.ds(h * H, H)

    def quarter(h, part_of):
        return pl.ds(h * H + part_of * (H // 2), H // 2)

    def chunk(j):
        return pl.ds(j * CR, CR)

    def piece_rows(j, h):
        return pl.ds(j * CR + h * HR, HR)

    own = blk(0, 1)
    shift = pl.multiple_of((y % 2) * (WIDE - PIECE), WIDE - PIECE)

    load_g = pltpu.make_async_copy(g_hbm, g_all.at[pl.ds(0, tok)], local.at[0])
    load_a = pltpu.make_async_copy(a_hbm, a_all.at[pl.ds(0, tok)], local.at[1])
    load_w = pltpu.make_async_copy(w_hbm.at[0], w_all.at[own], local.at[2])

    small = [
        pltpu.make_async_copy(src, dst, local.at[3 + i])
        for i, (src, dst) in enumerate(
            ((anchor_hbm, anchor_ref), (mom_hbm, mom_ref), (del_hbm, del_ref))
        )
    ]

    barrier = pltpu.get_barrier_semaphore()
    peers = [sib, zpeer, xpeer[1], xpeer[3], ypeer[1], ypeer[2], ypeer[3], lpeer]
    for p in peers:
        pl.semaphore_signal(barrier, inc=1, device_id=p, device_id_type=MESH)
    for cp in small:
        cp.start()
    load_g.start()
    load_a.start()
    load_w.start()
    pl.semaphore_wait(barrier, len(peers))

    go("SIBA", 0, a_hbm, a_all.at[pl.ds(tok, tok)], sib)
    go("SIBG", 0, g_hbm, g_all.at[pl.ds(tok, tok)], sib)
    for h in (0, 1):
        for way, k in ((0, 1), (1, 3)):
            hh = h if way == 0 else 1 - h
            go("AGX", way * 2 + hh, w_hbm.at[0, half(hh)], w_all.at[own, half(hh)], xpeer[k])
        go("AGZ", h, w_hbm.at[0, half(h)], w_all.at[own, half(h)], zpeer)

    pad[...] = jnp.zeros_like(pad)
    for cp in small:
        cp.wait()
    momentum = 0.9 * mom_ref[...] + del_ref[...]
    pad[pl.ds(shift, PIECE), :] = anchor_ref[...] - 0.7 * (del_ref[...] + 0.9 * momentum)
    an_all[rep] = pad[...].T.astype(BF)
    go("RAZ", 0, an_all.at[rep], an_all.at[rep], lpeer)
    for k in (1, 2, 3):
        go("RAY", k - 1, an_all.at[rep], an_all.at[rep], ypeer[k])

    load_a.wait()
    load_g.wait()
    got("SIBA", 0, a_hbm)
    got("SIBG", 0, g_hbm)

    def products(k):
        for zi in (0, 1):
            col = pl.multiple_of(fs_of(at_x(k), zh if zi else 1 - zh, c) * BLK, BLK)
            a_t[pl.ds(zi * BLK, BLK), :] = a_all[:, pl.ds(col, BLK)].T

        def step(n, carry):
            cols = pl.ds(pl.multiple_of(n * TILE_N, TILE_N), TILE_N)
            r = jnp.dot(a_t[...], g_all[:, cols], preferred_element_type=F32) * factor
            part[k, 0, :, cols] = r[:BLK].astype(BF)
            part[k, 1, :, cols] = r[BLK:].astype(BF)
            return carry

        lax.fori_loop(0, d // TILE_N, step, 0)

    def first(zi):
        for j in range(NJ):
            for h, k in ((0, 1), (1, 3)):
                go("RS1", rs_id(zi, j, h), part.at[2, zi, piece_rows(j, h)], rx1.at[zi, j, h], xpeer[k])

    def direct(zi, j):
        for h, k in ((1, 1), (0, 3)):
            go("RSD", rs_id(zi, j, h), part.at[k, zi, piece_rows(j, h)], rxd.at[zi, j, h], xpeer[k])

    def second(zi, j):
        for h, k in ((0, 1), (1, 3)):
            got("RS1", rs_id(zi, j, h), rx1.at[zi, j, h])
            sl = piece_rows(j, h)
            v = part[k, zi, sl, :].astype(F32) + rx1[zi, j, h].astype(F32)
            part[k, zi, sl, :] = v.astype(BF)
            go("RS2", rs_id(zi, j, h), part.at[k, zi, sl], rx2.at[zi, j, h], xpeer[k])

    def input_grad(slot, k, zi):
        b = blk(k, zi)

        def tile(r):
            return (
                lax.dot_general(
                    g_all[pl.ds(r, TILE_M), :], w_all[b], (((1,), (1,)), ((), ())),
                    preferred_element_type=F32,
                )
                * factor
            ).astype(BF)

        col = pl.multiple_of(fs_of(at_x(k), zh if zi else 1 - zh, c) * BLK, BLK)
        there = ig_ref.at[:, pl.ds(col, BLK)]
        for r in range(0, tok, TILE_M):
            ig_tx[slot, pl.ds(r, TILE_M), :] = tile(tok + r)
        go("IG", slot, ig_tx.at[slot], there, sib)
        for r in range(0, tok, TILE_M):
            ig_ref[pl.ds(r, TILE_M), pl.ds(col, BLK)] = tile(r)

    def to_z(way, h):
        ref = w_all.at[blk(3 if way == 0 else 1, 1), half(h)]
        got("AGX", way * 2 + h, ref)
        go("AGZ", 2 + way * 2 + h, ref, ref, zpeer)

    products(2)
    first(0)
    products(1)
    to_z(0, 0)
    to_z(1, 1)
    products(3)
    for j in range(NJ):
        direct(0, j)
    products(0)
    load_w.wait()
    to_z(0, 1)
    to_z(1, 0)

    for j in range(NJ):
        second(0, j)
    first(1)

    def onward(part_of):
        for way, k in ((0, 3), (1, 1)):
            ref = w_all.at[blk(k, 1), quarter(way, part_of)]
            go("AGF", way * 2 + part_of, ref, ref, xpeer[1 if way == 0 else 3])

    onward(0)

    got("RAZ", 0, an_all.at[lpeer[0]])
    for k in (1, 2, 3):
        ref = an_all.at[lpeer[0]]
        go("RAY", 3 + k - 1, ref, ref, ypeer[k])

    input_grad(0, 0, 1)
    input_grad(1, 1, 1)
    input_grad(2, 3, 1)

    for j in range(NJ):
        for h in (0, 1):
            got("RSD", rs_id(0, j, h), rxd.at[0, j, h])
            got("RS2", rs_id(0, j, h), rx2.at[0, j, h])
            sl = piece_rows(j, h)
            v = part[0, 0, sl, :].astype(F32) + rxd[0, j, h].astype(F32) + rx2[0, j, h].astype(F32)
            part[0, 0, sl, :] = v.astype(BF)
        go("RSZ", j, part.at[0, 0, chunk(j)], rxz.at[j], zpeer)

    for j in range(NJ):
        direct(1, j)
        second(1, j)
    onward(1)

    for h in (0, 1):
        got("AGZ", h, w_all.at[blk(0, 0), half(h)])
    later = []
    for way, k in ((0, 3), (1, 1)):
        for h in (0, 1):
            got("AGZ", 2 + way * 2 + h, w_all.at[blk(k, 0), half(h)])
        later.append((way, blk(k, 0)))
    for q in range(NQ):
        for way, b in later:
            ref = w_all.at[b, quarter(way, 1), pl.ds(q * (d // NQ), d // NQ)]
            go("AGY", way * NQ + q, ref, ref, xpeer[1 if way == 0 else 3])
    for h in (0, 1):
        ref = w_all.at[blk(2, 1), quarter(h, 0)]
        got("AGF", h * 2, ref)
        go("AGZ", 6 + h, ref, ref, zpeer)
    input_grad(3, 0, 0)
    input_grad(4, 1, 0)

    def piece(zz, yy):
        return pl.multiple_of(zz * 2304 + (yy // 2) * 1152 + (yy % 2) * 512, 128)

    def stepped(j):
        got("RSZ", j, rxz.at[j])
        for h in (0, 1):
            got("RSD", rs_id(1, j, h), rxd.at[1, j, h])
            got("RS2", rs_id(1, j, h), rx2.at[1, j, h])
            sl = piece_rows(j, h)
            v = (part[0, 1, sl, :].astype(F32) + rxd[1, j, h].astype(F32)) + (
                rx2[1, j, h].astype(F32) + rxz[j, pl.ds(h * HR, HR), :].astype(F32)
            )
            st[sl, :] = (w_all[own, sl, :].astype(F32) - v).astype(BF)
        for k in (1, 2, 3):
            for zz in (0, 1):
                col = piece(zz, (y + k) % 4)
                go(
                    "RRY", j * 6 + (k - 1) * 2 + zz,
                    st.at[chunk(j), pl.ds(col, WIDE)], ry.at[k - 1, zz, chunk(j)], ypeer[k],
                )

    def over_y(j):
        for k in (1, 2, 3):
            for zz in (0, 1):
                got("RRY", j * 6 + (k - 1) * 2 + zz, ry.at[k - 1, zz, chunk(j)])

        def total(zz):
            v = st[chunk(j), pl.ds(piece(zz, y), WIDE)].astype(F32)
            for k in range(3):
                v = v + ry[k, zz, chunk(j), :].astype(F32)
            return v

        tz[chunk(j), :] = total(1 - zl).astype(BF)
        go("RRZ", j, tz.at[chunk(j)], rzl.at[chunk(j)], lpeer)
        total_ref[chunk(j), :] = total(zl)

    for j in range(NJ):
        stepped(j)
        if j == 0:
            input_grad(5, 3, 0)
        else:
            over_y(j - 1)

    for k in (1, 2, 3):
        got("RAY", k - 1, an_all.at[rep])
        got("RAY", 3 + k - 1, an_all.at[rep])
    lane = lax.broadcasted_iota(jnp.int32, (16, 128), 1)

    def merge(i, carry):
        sl = pl.ds(pl.multiple_of(i * 16, 16), 16)
        for q in range(4):
            def put(lo, width, v):
                cols = pl.ds(q * 1152 + lo, width)
                ni_ref[0, sl, cols] = (0.5 * v + 0.5 * st[sl, cols].astype(F32)).astype(BF)

            even = an_all[2 * q, sl, :].astype(F32)
            odd = an_all[2 * q + 1, sl, :].astype(F32)
            put(0, 512, even[:, :512])
            put(512, 128, jnp.where(lane < 64, even[:, 512:], odd[:, :128]))
            put(640, 512, odd[:, 128:])
        return carry

    lax.fori_loop(0, BLK // 16, merge, 0)
    for m in sent:
        m.wait_send()
    over_y(NJ - 1)

    for h in (0, 1):
        got("AGF", h * 2 + 1, w_all.at[blk(2, 1), quarter(h, 1)])

    for h in (0, 1):
        got("AGZ", 6 + h, w_all.at[blk(2, 0), quarter(h, 0)])
    last = blk(2, 0)
    pair = pl.ds(at_x(2) * 2, 2)
    for q in range(NQ):
        cols = pl.ds(q * (d // NQ), d // NQ)
        for way in (0, 1):
            got("AGY", way * NQ + q, w_all.at[last, quarter(way, 1), cols])
        for r in (1, 0):
            sl = pl.ds(r * tok, tok)
            v = lax.dot_general(
                g_all[sl, cols], w_all[pair, :, cols].reshape(2 * BLK, d // NQ),
                (((1,), (1,)), ((), ())), preferred_element_type=F32,
            )
            if q > 0:
                v = v + acc[sl, :]
            if q < NQ - 1:
                acc[sl, :] = v
                continue
            v = (v * factor).astype(BF)
            for zz in (0, 1):
                col = pl.multiple_of(fs_of(at_x(2), zz, c) * BLK, BLK)
                there = pl.ds(col, BLK)
                if r:
                    ig_tx[6 + zz] = v[:, zz * BLK : (zz + 1) * BLK]
                    go("IG", 6 + zz, ig_tx.at[6 + zz], ig_ref.at[:, there], sib)
                else:
                    ig_ref[:, there] = v[:, zz * BLK : (zz + 1) * BLK]

    for j in range(NJ):
        got("RRZ", j, rzl.at[chunk(j)])
    pad[...] = (total_ref[...] + rzl[...].astype(F32)).T
    sum_ref[...] = pad[pl.ds(shift, PIECE), :]

    for slot in range(8):
        got("IG", slot, ig_tx.at[slot])
    for m in late:
        m.wait_send()


def finish(
    ig, ni, total, anchor, mom, delayed, ig_out, ni_out, na_out, nm_out, og_out,
    na_v, nm_v, og_v, sem,
):
    copies = [
        pltpu.make_async_copy(a, b, sem.at[i])
        for i, (a, b) in enumerate(
            [(nm_v, nm_out), (na_v, na_out), (og_v, og_out), (ni, ni_out)]
            + [(ig.at[pl.ds(r, 128)], ig_out.at[pl.ds(r, 128)]) for r in range(0, 512, 128)]
        )
    ]
    for cp in copies[3:]:
        cp.start()
    momentum = 0.9 * mom[...] + delayed[...]
    nm_v[...] = momentum
    copies[0].start()
    na_v[...] = anchor[...] - 0.7 * (delayed[...] + 0.9 * momentum)
    copies[1].start()
    og_v[...] = anchor[...] - total[...] * 0.125
    copies[2].start()
    for cp in copies:
        cp.wait()


def per_device(attn_out, grad_out, inner_w, anchor, momentum, delayed):
    tok, d = grad_out.shape
    hd = attn_out.shape[1]
    hbm = pl.BlockSpec(memory_space=pl.ANY)
    vm = pl.BlockSpec(memory_space=pltpu.VMEM)
    shape = jax.ShapeDtypeStruct
    across = (anchor.T, momentum.T, delayed.T)
    input_grad, new_inner, summed = pl.pallas_call(
        kernel,
        out_shape=(
            pltpu.VMEM((tok, hd), BF), pltpu.VMEM(inner_w.shape, BF), pltpu.VMEM((PIECE, BLK), F32)
        ),
        in_specs=[hbm] * 6,
        out_specs=(vm,) * 3,
        scratch_shapes=[
            pltpu.VMEM((8, BLK, d), BF),
            pltpu.VMEM((2 * tok, d), BF),
            pltpu.VMEM((2 * tok, hd), BF),
            pltpu.VMEM((2 * BLK, 2 * tok), BF),
            pltpu.VMEM((4, 2, BLK, d), BF),
            pltpu.VMEM((2, NJ, 2, HR, d), BF),
            pltpu.VMEM((2, NJ, 2, HR, d), BF),
            pltpu.VMEM((2, NJ, 2, HR, d), BF),
            pltpu.VMEM((NJ, CR, d), BF),
            pltpu.VMEM((8, tok, BLK), BF),
            pltpu.VMEM((BLK, d), BF),
            pltpu.VMEM((8, BLK, WIDE), BF),
            pltpu.VMEM((3, 2, BLK, WIDE), BF),
            pltpu.VMEM((BLK, WIDE), BF),
            pltpu.VMEM((BLK, WIDE), BF),
            pltpu.VMEM((BLK, WIDE), F32),
            pltpu.VMEM((WIDE, BLK), F32),
            pltpu.VMEM((PIECE, BLK), F32),
            pltpu.VMEM((PIECE, BLK), F32),
            pltpu.VMEM((PIECE, BLK), F32),
            pltpu.VMEM((2 * tok, 2 * BLK), F32),
            pltpu.SemaphoreType.DMA((N_MSG,)),
            pltpu.SemaphoreType.DMA((N_MSG,)),
            pltpu.SemaphoreType.DMA((6,)),
        ],
        compiler_params=pltpu.CompilerParams(
            collective_id=0, has_side_effects=True, vmem_limit_bytes=57 * 2**20
        ),
    )(attn_out, grad_out, inner_w, *across)
    f32 = shape((PIECE, BLK), F32)
    input_grad, new_inner, *rest = pl.pallas_call(
        finish,
        out_shape=(shape((tok, hd), BF), shape(inner_w.shape, BF), f32, f32, f32),
        in_specs=[vm] * 6,
        out_specs=(hbm,) * 5,
        scratch_shapes=[pltpu.VMEM((PIECE, BLK), F32)] * 3 + [pltpu.SemaphoreType.DMA((8,))],
        compiler_params=pltpu.CompilerParams(vmem_limit_bytes=16 * 2**20),
    )(input_grad, new_inner, summed, *across)
    return (input_grad, new_inner, *(v.T for v in rest))


def solution(mesh):
    return jax.shard_map(
        per_device,
        mesh=mesh,
        in_specs=(
            P(("rep", "fsdp"), None),
            P(("rep", "fsdp"), None),
            P("rep", "fsdp", None),
            P("fsdp", "rep"),
            P("fsdp", "rep"),
            P("fsdp", "rep"),
        ),
        out_specs=(
            P(("rep", "fsdp"), None),
            P("rep", "fsdp", None),
            P("fsdp", "rep"),
            P("fsdp", "rep"),
            P("fsdp", "rep"),
        ),
        check_vma=False,
    )
```

```python
import functools

import jax
import jax.numpy as jnp
from jax import lax
from jax.experimental import pallas as pl
from jax.experimental.pallas import tpu as pltpu
from jax.sharding import PartitionSpec as P

MESH = pl.DeviceIdType.MESH
BF = jnp.bfloat16
F32 = jnp.float32

BLK = 128
H = 64
NJ = 4
CR = BLK // NJ
HR = CR // 2
TILE_N = 1536
TILE_M = 512
NQ = 6
PIECE = 576
WIDE = 640


def numbers(**counts):
    first, at = {}, 0
    for name, count in counts.items():
        first[name] = at
        at += count
    return first, at


FIRST, N_MSG = numbers(
    AGX=4, AGF=4, AGZ=8, AGY=2 * NQ, RS1=4 * NJ, RSD=4 * NJ, RS2=4 * NJ, RSZ=NJ, SIBG=1, SIBA=1, IG=8,
    RAZ=1, RAY=6, RRY=6 * NJ, RRZ=NJ,
)


def kernel(
    a_hbm, g_hbm, w_hbm, anchor_hbm, mom_hbm, del_hbm,
    ig_ref, ni_ref, sum_ref,
    w_all, g_all, a_all, a_t, part, rx1, rxd, rx2, rxz,
    ig_tx, st, an_all, ry, tz, rzl, total_ref, pad,
    anchor_ref, mom_ref, del_ref, acc,
    send, recv, local,
):
    d = g_hbm.shape[1]
    tok = g_hbm.shape[0]
    factor = d ** (-0.5)
    rep = lax.axis_index("rep")
    fs = lax.axis_index("fsdp")
    x, zh, c = fs // 4, (fs // 2) % 2, fs % 2
    zl, y = rep // 4, rep % 4

    def at_x(k):
        return (x + k) % 4

    def fs_of(xx, zz, cc):
        return xx * 4 + zz * 2 + cc

    sib = (rep, fs_of(x, zh, 1 - c))
    zpeer = (rep, fs_of(x, 1 - zh, c))
    xpeer = {k: (rep, fs_of(at_x(k), zh, c)) for k in (1, 3)}
    ypeer = {k: (zl * 4 + (y + k) % 4, fs) for k in (1, 2, 3)}
    lpeer = ((1 - zl) * 4 + y, fs)

    def blk(k, zi):
        return at_x(k) * 2 + (zh if zi else 1 - zh)

    def msg(name, i, src, dst, dev):
        n = FIRST[name] + i
        return pltpu.make_async_remote_copy(
            src_ref=src, dst_ref=dst, send_sem=send.at[n], recv_sem=recv.at[n],
            device_id=dev, device_id_type=MESH,
        )

    sent, late = [], []

    def rs_id(zi, j, h):
        return (zi * NJ + j) * 2 + h

    def go(name, i, src, dst, dev):
        m = msg(name, i, src, dst, dev)
        m.start()
        last = (
            name in ("AGY", "RRZ")
            or (name == "AGZ" and i >= 6)
            or (name == "AGF" and i % 2 == 1)
            or (name == "RRY" and i >= 6 * (NJ - 1))
            or (name in ("RSD", "RS2") and i >= rs_id(1, NJ - 1, 0))
            or (name == "IG" and i >= 5)
        )
        (late if last else sent).append(m)

    def got(name, i, ref):
        msg(name, i, ref, ref, sib).wait_recv()

    def half(h):
        return pl.ds(h * H, H)

    def quarter(h, part_of):
        return pl.ds(h * H + part_of * (H // 2), H // 2)

    def chunk(j):
        return pl.ds(j * CR, CR)

    def piece_rows(j, h):
        return pl.ds(j * CR + h * HR, HR)

    own = blk(0, 1)
    shift = pl.multiple_of((y % 2) * (WIDE - PIECE), WIDE - PIECE)

    load_g = pltpu.make_async_copy(g_hbm, g_all.at[pl.ds(0, tok)], local.at[0])
    load_a = pltpu.make_async_copy(a_hbm, a_all.at[pl.ds(0, tok)], local.at[1])
    load_w = pltpu.make_async_copy(w_hbm.at[0], w_all.at[own], local.at[2])

    small = [
        pltpu.make_async_copy(src, dst, local.at[3 + i])
        for i, (src, dst) in enumerate(
            ((anchor_hbm, anchor_ref), (mom_hbm, mom_ref), (del_hbm, del_ref))
        )
    ]

    barrier = pltpu.get_barrier_semaphore()
    peers = [sib, zpeer, xpeer[1], xpeer[3], ypeer[1], ypeer[2], ypeer[3], lpeer]
    for p in peers:
        pl.semaphore_signal(barrier, inc=1, device_id=p, device_id_type=MESH)
    for cp in small:
        cp.start()
    load_g.start()
    load_a.start()
    load_w.start()
    pl.semaphore_wait(barrier, len(peers))

    go("SIBA", 0, a_hbm, a_all.at[pl.ds(tok, tok)], sib)
    go("SIBG", 0, g_hbm, g_all.at[pl.ds(tok, tok)], sib)
    for h in (0, 1):
        for way, k in ((0, 1), (1, 3)):
            hh = h if way == 0 else 1 - h
            go("AGX", way * 2 + hh, w_hbm.at[0, half(hh)], w_all.at[own, half(hh)], xpeer[k])
        go("AGZ", h, w_hbm.at[0, half(h)], w_all.at[own, half(h)], zpeer)

    pad[...] = jnp.zeros_like(pad)
    for cp in small:
        cp.wait()
    momentum = 0.9 * mom_ref[...] + del_ref[...]
    pad[pl.ds(shift, PIECE), :] = anchor_ref[...] - 0.7 * (del_ref[...] + 0.9 * momentum)
    an_all[rep] = pad[...].T.astype(BF)
    go("RAZ", 0, an_all.at[rep], an_all.at[rep], lpeer)
    for k in (1, 2, 3):
        go("RAY", k - 1, an_all.at[rep], an_all.at[rep], ypeer[k])

    load_a.wait()
    load_g.wait()
    got("SIBA", 0, a_hbm)
    got("SIBG", 0, g_hbm)

    def products(k):
        for zi in (0, 1):
            col = pl.multiple_of(fs_of(at_x(k), zh if zi else 1 - zh, c) * BLK, BLK)
            a_t[pl.ds(zi * BLK, BLK), :] = a_all[:, pl.ds(col, BLK)].T

        def step(n, carry):
            cols = pl.ds(pl.multiple_of(n * TILE_N, TILE_N), TILE_N)
            r = jnp.dot(a_t[...], g_all[:, cols], preferred_element_type=F32) * factor
            part[k, 0, :, cols] = r[:BLK].astype(BF)
            part[k, 1, :, cols] = r[BLK:].astype(BF)
            return carry

        lax.fori_loop(0, d // TILE_N, step, 0)

    def first(zi):
        for j in range(NJ):
            for h, k in ((0, 1), (1, 3)):
                go("RS1", rs_id(zi, j, h), part.at[2, zi, piece_rows(j, h)], rx1.at[zi, j, h], xpeer[k])

    def direct(zi, j):
        for h, k in ((1, 1), (0, 3)):
            go("RSD", rs_id(zi, j, h), part.at[k, zi, piece_rows(j, h)], rxd.at[zi, j, h], xpeer[k])

    def second(zi, j):
        for h, k in ((0, 1), (1, 3)):
            got("RS1", rs_id(zi, j, h), rx1.at[zi, j, h])
            sl = piece_rows(j, h)
            v = part[k, zi, sl, :].astype(F32) + rx1[zi, j, h].astype(F32)
            part[k, zi, sl, :] = v.astype(BF)
            go("RS2", rs_id(zi, j, h), part.at[k, zi, sl], rx2.at[zi, j, h], xpeer[k])

    def input_grad(slot, k, zi):
        b = blk(k, zi)

        def tile(r):
            return (
                lax.dot_general(
                    g_all[pl.ds(r, TILE_M), :], w_all[b], (((1,), (1,)), ((), ())),
                    preferred_element_type=F32,
                )
                * factor
            ).astype(BF)

        col = pl.multiple_of(fs_of(at_x(k), zh if zi else 1 - zh, c) * BLK, BLK)
        there = ig_ref.at[:, pl.ds(col, BLK)]
        for r in range(0, tok, TILE_M):
            ig_tx[slot, pl.ds(r, TILE_M), :] = tile(tok + r)
        go("IG", slot, ig_tx.at[slot], there, sib)
        for r in range(0, tok, TILE_M):
            ig_ref[pl.ds(r, TILE_M), pl.ds(col, BLK)] = tile(r)

    def to_z(way, h):
        ref = w_all.at[blk(3 if way == 0 else 1, 1), half(h)]
        got("AGX", way * 2 + h, ref)
        go("AGZ", 2 + way * 2 + h, ref, ref, zpeer)

    products(2)
    first(0)
    products(1)
    to_z(0, 0)
    to_z(1, 1)
    products(3)
    for j in range(NJ):
        direct(0, j)
    products(0)
    load_w.wait()
    to_z(0, 1)
    to_z(1, 0)

    for j in range(NJ):
        second(0, j)
    first(1)

    def onward(part_of):
        for way, k in ((0, 3), (1, 1)):
            ref = w_all.at[blk(k, 1), quarter(way, part_of)]
            go("AGF", way * 2 + part_of, ref, ref, xpeer[1 if way == 0 else 3])

    onward(0)

    got("RAZ", 0, an_all.at[lpeer[0]])
    for k in (1, 2, 3):
        ref = an_all.at[lpeer[0]]
        go("RAY", 3 + k - 1, ref, ref, ypeer[k])

    input_grad(0, 0, 1)
    input_grad(1, 1, 1)
    input_grad(2, 3, 1)

    for j in range(NJ):
        for h in (0, 1):
            got("RSD", rs_id(0, j, h), rxd.at[0, j, h])
            got("RS2", rs_id(0, j, h), rx2.at[0, j, h])
            sl = piece_rows(j, h)
            v = part[0, 0, sl, :].astype(F32) + rxd[0, j, h].astype(F32) + rx2[0, j, h].astype(F32)
            part[0, 0, sl, :] = v.astype(BF)
        go("RSZ", j, part.at[0, 0, chunk(j)], rxz.at[j], zpeer)

    for j in range(NJ):
        direct(1, j)
        second(1, j)
    onward(1)

    for h in (0, 1):
        got("AGZ", h, w_all.at[blk(0, 0), half(h)])
    later = []
    for way, k in ((0, 3), (1, 1)):
        for h in (0, 1):
            got("AGZ", 2 + way * 2 + h, w_all.at[blk(k, 0), half(h)])
        later.append((way, blk(k, 0)))
    for q in range(NQ):
        for way, b in later:
            ref = w_all.at[b, quarter(way, 1), pl.ds(q * (d // NQ), d // NQ)]
            go("AGY", way * NQ + q, ref, ref, xpeer[1 if way == 0 else 3])
    for h in (0, 1):
        ref = w_all.at[blk(2, 1), quarter(h, 0)]
        got("AGF", h * 2, ref)
        go("AGZ", 6 + h, ref, ref, zpeer)
    input_grad(3, 0, 0)
    input_grad(4, 1, 0)

    def piece(zz, yy):
        return pl.multiple_of(zz * 2304 + (yy // 2) * 1152 + (yy % 2) * 512, 128)

    def stepped(j):
        got("RSZ", j, rxz.at[j])
        for h in (0, 1):
            got("RSD", rs_id(1, j, h), rxd.at[1, j, h])
            got("RS2", rs_id(1, j, h), rx2.at[1, j, h])
            sl = piece_rows(j, h)
            v = (part[0, 1, sl, :].astype(F32) + rxd[1, j, h].astype(F32)) + (
                rx2[1, j, h].astype(F32) + rxz[j, pl.ds(h * HR, HR), :].astype(F32)
            )
            st[sl, :] = (w_all[own, sl, :].astype(F32) - v).astype(BF)
        for k in (1, 2, 3):
            for zz in (0, 1):
                col = piece(zz, (y + k) % 4)
                go(
                    "RRY", j * 6 + (k - 1) * 2 + zz,
                    st.at[chunk(j), pl.ds(col, WIDE)], ry.at[k - 1, zz, chunk(j)], ypeer[k],
                )

    def over_y(j):
        for k in (1, 2, 3):
            for zz in (0, 1):
                got("RRY", j * 6 + (k - 1) * 2 + zz, ry.at[k - 1, zz, chunk(j)])

        def total(zz):
            v = st[chunk(j), pl.ds(piece(zz, y), WIDE)].astype(F32)
            for k in range(3):
                v = v + ry[k, zz, chunk(j), :].astype(F32)
            return v

        tz[chunk(j), :] = total(1 - zl).astype(BF)
        go("RRZ", j, tz.at[chunk(j)], rzl.at[chunk(j)], lpeer)
        total_ref[chunk(j), :] = total(zl)

    for j in range(NJ):
        stepped(j)
        if j == 0:
            input_grad(5, 3, 0)
        else:
            over_y(j - 1)

    for k in (1, 2, 3):
        got("RAY", k - 1, an_all.at[rep])
        got("RAY", 3 + k - 1, an_all.at[rep])
    lane = lax.broadcasted_iota(jnp.int32, (16, 128), 1)

    def merge(i, carry):
        sl = pl.ds(pl.multiple_of(i * 16, 16), 16)
        for q in range(4):
            def put(lo, width, v):
                cols = pl.ds(q * 1152 + lo, width)
                ni_ref[0, sl, cols] = (0.5 * v + 0.5 * st[sl, cols].astype(F32)).astype(BF)

            even = an_all[2 * q, sl, :].astype(F32)
            odd = an_all[2 * q + 1, sl, :].astype(F32)
            put(0, 512, even[:, :512])
            put(512, 128, jnp.where(lane < 64, even[:, 512:], odd[:, :128]))
            put(640, 512, odd[:, 128:])
        return carry

    lax.fori_loop(0, BLK // 16, merge, 0)
    for m in sent:
        m.wait_send()
    over_y(NJ - 1)

    for h in (0, 1):
        got("AGF", h * 2 + 1, w_all.at[blk(2, 1), quarter(h, 1)])

    for h in (0, 1):
        got("AGZ", 6 + h, w_all.at[blk(2, 0), quarter(h, 0)])
    last = blk(2, 0)
    pair = pl.ds(at_x(2) * 2, 2)
    for q in range(NQ):
        cols = pl.ds(q * (d // NQ), d // NQ)
        for way in (0, 1):
            got("AGY", way * NQ + q, w_all.at[last, quarter(way, 1), cols])
        for r in (1, 0):
            sl = pl.ds(r * tok, tok)
            v = lax.dot_general(
                g_all[sl, cols], w_all[pair, :, cols].reshape(2 * BLK, d // NQ),
                (((1,), (1,)), ((), ())), preferred_element_type=F32,
            )
            if q > 0:
                v = v + acc[sl, :]
            if q < NQ - 1:
                acc[sl, :] = v
                continue
            v = (v * factor).astype(BF)
            for zz in (0, 1):
                col = pl.multiple_of(fs_of(at_x(2), zz, c) * BLK, BLK)
                there = pl.ds(col, BLK)
                if r:
                    ig_tx[6 + zz] = v[:, zz * BLK : (zz + 1) * BLK]
                    go("IG", 6 + zz, ig_tx.at[6 + zz], ig_ref.at[:, there], sib)
                else:
                    ig_ref[:, there] = v[:, zz * BLK : (zz + 1) * BLK]

    for j in range(NJ):
        got("RRZ", j, rzl.at[chunk(j)])
    pad[...] = (total_ref[...] + rzl[...].astype(F32)).T
    sum_ref[...] = pad[pl.ds(shift, PIECE), :]

    for slot in range(8):
        got("IG", slot, ig_tx.at[slot])
    for m in late:
        m.wait_send()


def finish(
    ig, ni, total, anchor, mom, delayed, ig_out, ni_out, na_out, nm_out, og_out,
    na_v, nm_v, og_v, sem,
):
    copies = [
        pltpu.make_async_copy(a, b, sem.at[i])
        for i, (a, b) in enumerate(
            [(nm_v, nm_out), (na_v, na_out), (og_v, og_out), (ni, ni_out)]
            + [(ig.at[pl.ds(r, 128)], ig_out.at[pl.ds(r, 128)]) for r in range(0, 512, 128)]
        )
    ]
    for cp in copies[3:]:
        cp.start()
    momentum = 0.9 * mom[...] + delayed[...]
    nm_v[...] = momentum
    copies[0].start()
    na_v[...] = anchor[...] - 0.7 * (delayed[...] + 0.9 * momentum)
    copies[1].start()
    og_v[...] = anchor[...] - total[...] * 0.125
    copies[2].start()
    for cp in copies:
        cp.wait()


def per_device(attn_out, grad_out, inner_w, anchor, momentum, delayed):
    tok, d = grad_out.shape
    hd = attn_out.shape[1]
    hbm = pl.BlockSpec(memory_space=pl.ANY)
    vm = pl.BlockSpec(memory_space=pltpu.VMEM)
    shape = jax.ShapeDtypeStruct
    across = (anchor.T, momentum.T, delayed.T)
    input_grad, new_inner, summed = pl.pallas_call(
        kernel,
        out_shape=(
            pltpu.VMEM((tok, hd), BF), pltpu.VMEM(inner_w.shape, BF), pltpu.VMEM((PIECE, BLK), F32)
        ),
        in_specs=[hbm] * 6,
        out_specs=(vm,) * 3,
        scratch_shapes=[
            pltpu.VMEM((8, BLK, d), BF),
            pltpu.VMEM((2 * tok, d), BF),
            pltpu.VMEM((2 * tok, hd), BF),
            pltpu.VMEM((2 * BLK, 2 * tok), BF),
            pltpu.VMEM((4, 2, BLK, d), BF),
            pltpu.VMEM((2, NJ, 2, HR, d), BF),
            pltpu.VMEM((2, NJ, 2, HR, d), BF),
            pltpu.VMEM((2, NJ, 2, HR, d), BF),
            pltpu.VMEM((NJ, CR, d), BF),
            pltpu.VMEM((8, tok, BLK), BF),
            pltpu.VMEM((BLK, d), BF),
            pltpu.VMEM((8, BLK, WIDE), BF),
            pltpu.VMEM((3, 2, BLK, WIDE), BF),
            pltpu.VMEM((BLK, WIDE), BF),
            pltpu.VMEM((BLK, WIDE), BF),
            pltpu.VMEM((BLK, WIDE), F32),
            pltpu.VMEM((WIDE, BLK), F32),
            pltpu.VMEM((PIECE, BLK), F32),
            pltpu.VMEM((PIECE, BLK), F32),
            pltpu.VMEM((PIECE, BLK), F32),
            pltpu.VMEM((2 * tok, 2 * BLK), F32),
            pltpu.SemaphoreType.DMA((N_MSG,)),
            pltpu.SemaphoreType.DMA((N_MSG,)),
            pltpu.SemaphoreType.DMA((6,)),
        ],
        compiler_params=pltpu.CompilerParams(
            collective_id=0, has_side_effects=True, vmem_limit_bytes=57 * 2**20
        ),
    )(attn_out, grad_out, inner_w, *across)
    f32 = shape((PIECE, BLK), F32)
    input_grad, new_inner, *rest = pl.pallas_call(
        finish,
        out_shape=(shape((tok, hd), BF), shape(inner_w.shape, BF), f32, f32, f32),
        in_specs=[vm] * 6,
        out_specs=(hbm,) * 5,
        scratch_shapes=[pltpu.VMEM((PIECE, BLK), F32)] * 3 + [pltpu.SemaphoreType.DMA((8,))],
        compiler_params=pltpu.CompilerParams(vmem_limit_bytes=16 * 2**20),
    )(input_grad, new_inner, summed, *across)
    return (input_grad, new_inner, *(v.T for v in rest))


def solution(mesh):
    return jax.shard_map(
        per_device,
        mesh=mesh,
        in_specs=(
            P(("rep", "fsdp"), None),
            P(("rep", "fsdp"), None),
            P("rep", "fsdp", None),
            P("fsdp", "rep"),
            P("fsdp", "rep"),
            P("fsdp", "rep"),
        ),
        out_specs=(
            P(("rep", "fsdp"), None),
            P("rep", "fsdp", None),
            P("fsdp", "rep"),
            P("fsdp", "rep"),
            P("fsdp", "rep"),
        ),
        check_vma=False,
    )
```
